32 devices in a mesh: seq: 8 (over y, x, core), tensor: 4 (over z).
Axes of the slice: x: 2, y: 2, z: 4, core: 2. Of those that a mesh axis runs over, the one named last changes fastest.
Arguments:
- inputs: bfloat16 [1, 1024, 4096], P(None, 'seq', 'tensor'), may hold values from -6 to 6
- projections: bfloat16 [1, 1024, 1024], P(None, 'seq', 'tensor'), may hold values from -4 to 4
- step_raw: float32 [64, 1, 1024], P('tensor', None, 'seq'), may hold values from -16 to 1.2, as said below
- rate_log: float32 [64], P('tensor'), may hold values from -0.7 to 0.7
- out_grad: bfloat16 [1, 1024, 4096], P(None, 'seq', 'tensor'), may hold values from -24 to 24
Outputs:
- grad_inputs: bfloat16 [1, 1024, 4096], P(None, 'seq', 'tensor')
- grad_projections: bfloat16 [1, 1024, 1024], P(None, 'seq', 'tensor')
- grad_step_raw: float32 [64, 1, 1024], P('tensor', None, 'seq')
- grad_rate_log: float32 [64], P('tensor')
The draws below stay inside these ranges and needn't reach their ends.
Inputs may be any that keep to these rules, and one draw needn't show every extreme that they name: `step_raw`: log(exp(step) - 1) of a positive step size.
All inputs are finite; a program needn't handle non-finite values.
Results may differ from the reference program's by a relative error of at most 0.001.
Values may be sent and summed in bfloat16 or wider, within the bound.
A program may use at most 192 MiB of HBM per device.

```python
import math
import jax
import jax.numpy as jnp
from jax import lax

P_SIZE = 64
N = 256
SPAN = 128
HEAD_DEV = 16
SEQUENCE_COUNT = 1
HEADS = 64
GROUPS = 2
SEQUENCE_LENGTH = 1024


def step_law(key, share):
    random_keys = jax.random.split(key, 8)
    fast = jax.random.uniform(random_keys[0], (HEADS,)) < share
    slow_rate = jnp.exp(jax.random.uniform(random_keys[1], (HEADS,), minval=math.log(0.25), maxval=math.log(0.5))) / SEQUENCE_LENGTH
    fast_rate = jnp.exp(jax.random.uniform(random_keys[2], (HEADS,), minval=math.log(0.02), maxval=math.log(0.04)))
    rate = jnp.where(fast, fast_rate, slow_rate)
    value_scale = jnp.exp(jax.random.uniform(random_keys[3], (HEADS,), minval=-0.69, maxval=0.69))
    rough = jnp.exp(jax.random.uniform(random_keys[4], (HEADS, SEQUENCE_COUNT, SEQUENCE_LENGTH), minval=-0.7, maxval=0.7))
    blocky = jnp.exp(jax.random.uniform(random_keys[5], (HEADS, SEQUENCE_COUNT, SEQUENCE_LENGTH // SPAN, 1), minval=-0.35, maxval=0.35))
    blocky = jnp.broadcast_to(blocky, (HEADS, SEQUENCE_COUNT, SEQUENCE_LENGTH // SPAN, SPAN)).reshape(HEADS, SEQUENCE_COUNT, SEQUENCE_LENGTH)
    step_width = rate[:, None, None] * rough * blocky / value_scale[:, None, None]
    block_span = jax.random.uniform(random_keys[6], (SEQUENCE_COUNT, SEQUENCE_LENGTH)) < 3.0 / SEQUENCE_LENGTH
    block_length = jnp.exp(jax.random.uniform(random_keys[7], (SEQUENCE_COUNT, SEQUENCE_LENGTH), minval=math.log(0.25), maxval=math.log(0.7)))
    step_width = jnp.where(block_span[None], block_length[None] / value_scale[:, None, None], step_width)
    return (step_width, value_scale)


def draw_step_raw(key, part):
    share = 0.5
    step_width, value_scale = step_law(key, share)
    return jnp.log(jnp.expm1(step_width)).astype(jnp.float32)


def draw_rate_log(key, part):
    share = 0.5
    step_width, value_scale = step_law(key, share)
    return jnp.log(value_scale).astype(jnp.float32)


def steps_of(rng, dims, cuts, low, largest):
    gain = 1.0
    for axis_at, blocks in cuts:
        draws = jax.random.uniform(jax.random.fold_in(jax.random.fold_in(rng, 6), axis_at), (blocks,), jnp.float32, low / len(cuts), largest / len(cuts))
        gain = gain * jnp.repeat(jnp.exp(draws), dims[axis_at] // blocks).reshape((-1,) + (1,) * (len(dims) - 1 - axis_at))
    return gain


def centred(key, dims, spread, limit, cuts=(), kind=jnp.bfloat16):
    result = spread * jax.random.normal(key, dims, jnp.float32)
    if cuts:
        result = result * steps_of(key, dims, cuts, -0.22, 0.18)
    return jnp.clip(result, -limit, limit).astype(kind)


def setup_inputs(seed: int = 0) -> dict:
    key_of = jax.random.split(jax.random.key(seed), 6)
    return {
        "inputs": centred(key_of[0], (SEQUENCE_COUNT, SEQUENCE_LENGTH, HEADS * P_SIZE), 1.0, 6.0, ((1, 8), (2, 4))),
        "projections": centred(key_of[1], (SEQUENCE_COUNT, SEQUENCE_LENGTH, GROUPS * 2 * N), 0.3, 4.0, ((1, 8), (2, 4))),
        "step_raw": draw_step_raw(jax.random.fold_in(key_of[5], 71), 0),
        "rate_log": draw_rate_log(jax.random.fold_in(key_of[5], 71), 0),
        "out_grad": centred(key_of[4], (SEQUENCE_COUNT, SEQUENCE_LENGTH, HEADS * P_SIZE), 4.0, 24.0, ((1, 8), (2, 4))),
    }


HIGHEST = lax.Precision.HIGHEST

def segment_forward(scaled, inject, readout, log_decay, entering):
    seq_count, tok_count, head_count, head_width = scaled.shape
    state_width = inject.shape[-1]
    blocks = tok_count // SPAN
    scaled_blocks = scaled.reshape(seq_count, blocks, SPAN, head_count, head_width).transpose(1, 0, 2, 3, 4)
    inject_blocks = inject.reshape(seq_count, blocks, SPAN, state_width).transpose(1, 0, 2, 3)
    readout_blocks = readout.reshape(seq_count, blocks, SPAN, state_width).transpose(1, 0, 2, 3)
    decay_blocks = log_decay.reshape(seq_count, head_count, blocks, SPAN).transpose(2, 0, 1, 3)
    position = jnp.arange(SPAN)
    causal = position[:, None] >= position[None, :]

    def advance(running, pieces):
        scaled_piece, inject_piece, readout_piece, decay_piece = pieces
        cumulative = jnp.cumsum(decay_piece, axis=-1)
        scores = jnp.einsum('sin,sjn->sij', readout_piece, inject_piece, precision=HIGHEST)
        log_gap = jnp.where(causal, cumulative[..., :, None] - cumulative[..., None, :], 0.0)
        weight = jnp.where(causal, jnp.exp(log_gap), 0.0) * scores[:, None]
        within = jnp.einsum('shij,sjhp->sihp', weight, scaled_piece, precision=HIGHEST)
        carried = jnp.einsum('sin,shpn->sihp', readout_piece, running, precision=HIGHEST)
        carried = carried * jnp.exp(cumulative).transpose(0, 2, 1)[..., None]
        to_end = jnp.exp(cumulative[..., -1:] - cumulative)
        updated = jnp.exp(cumulative[..., -1])[..., None, None] * running
        updated = updated + jnp.einsum('shj,sjhp,sjn->shpn', to_end, scaled_piece, inject_piece, precision=HIGHEST)
        return (updated, within + carried)
    closing, outputs = lax.scan(advance, entering, (scaled_blocks, inject_blocks, readout_blocks, decay_blocks))
    outputs = outputs.transpose(1, 0, 2, 3, 4).reshape(seq_count, tok_count, head_count, head_width)
    return (outputs, closing)

def prepare(values, step_raw, rate_log):
    step_width = jax.nn.softplus(step_raw)
    log_decay = step_width.transpose(1, 0, 2) * (-jnp.exp(rate_log))[None, :, None]
    scaled = values * step_width.transpose(1, 2, 0)[..., None]
    return (scaled, log_decay)

def group_grads(group, inputs, projections, step_raw, rate_log, out_grad):
    group_heads = 2 * HEAD_DEV
    first = (group * group_heads).astype(jnp.int32)
    column = (group * group_heads * P_SIZE).astype(jnp.int32)
    values = lax.dynamic_slice_in_dim(inputs, column, group_heads * P_SIZE, 2).astype(jnp.float32)
    values = values.reshape(SEQUENCE_COUNT, SEQUENCE_LENGTH, group_heads, P_SIZE)
    cotangent = lax.dynamic_slice_in_dim(out_grad, column, group_heads * P_SIZE, 2).astype(jnp.float32)
    cotangent = cotangent.reshape(SEQUENCE_COUNT, SEQUENCE_LENGTH, group_heads, P_SIZE)
    pair = lax.dynamic_slice_in_dim(projections, (group * 2 * N).astype(jnp.int32), 2 * N, 2).astype(jnp.float32)
    inject = pair[..., :N]
    readout = pair[..., N:]
    steps_here = lax.dynamic_slice_in_dim(step_raw, first, group_heads, 0)
    rates_here = lax.dynamic_slice_in_dim(rate_log, first, group_heads, 0)

    def forward(values, inject, readout, steps_here, rates_here):
        scaled, log_decay = prepare(values, steps_here, rates_here)
        empty_state = jnp.zeros((SEQUENCE_COUNT, group_heads, P_SIZE, N), jnp.float32)
        return segment_forward(scaled, inject, readout, log_decay, empty_state)[0]
    _, pull = jax.vjp(forward, values, inject, readout, steps_here, rates_here)
    grad_values, grad_inject, grad_readout, grad_steps, grad_rates = pull(cotangent)
    grad_values = grad_values.reshape(SEQUENCE_COUNT, SEQUENCE_LENGTH, group_heads * P_SIZE).astype(jnp.bfloat16)
    grad_pair = jnp.stack([grad_inject, grad_readout], 2).astype(jnp.bfloat16)
    return (grad_values, grad_pair, grad_steps, grad_rates)

def reference(inputs, projections, step_raw, rate_log, out_grad):

    def one_group(group):
        return group_grads(group, inputs, projections, step_raw, rate_log, out_grad)
    grad_values, grad_pair, grad_steps, grad_rates = lax.map(one_group, jnp.arange(GROUPS, dtype=jnp.int32))
    grad_inputs = grad_values.transpose(1, 2, 0, 3).reshape(SEQUENCE_COUNT, SEQUENCE_LENGTH, HEADS * P_SIZE)
    grad_projections = grad_pair.transpose(1, 2, 0, 3, 4).reshape(SEQUENCE_COUNT, SEQUENCE_LENGTH, GROUPS * 2 * N)
    grad_step_raw = grad_steps.reshape(HEADS, SEQUENCE_COUNT, SEQUENCE_LENGTH)
    grad_rate_log = grad_rates.reshape(HEADS)
    return (grad_inputs, grad_projections, grad_step_raw, grad_rate_log)
```

```python
import functools

import jax
import jax.numpy as jnp
from jax import lax
from jax.experimental import pallas as pl
from jax.experimental.pallas import tpu as pltpu
from jax.sharding import PartitionSpec as P

MESH = pl.DeviceIdType.MESH
HIGHEST = lax.Precision.HIGHEST
F32, BF16 = jnp.float32, jnp.bfloat16
CHUNK = 256
NT = (((1,), (1,)), ((), ()))
TN = (((0,), (0,)), ((), ()))
NN = (((1,), (0,)), ((), ()))


def dot(a, b, dims=NN):
    return lax.dot_general(a, b, dims, preferred_element_type=F32)


def split(a):
    high = a.astype(BF16)
    return high, (a - high.astype(F32)).astype(BF16)


def kernel(seq_count, head_width, x_ref, proj_ref, raw_ref, rate_ref, g_ref,
           gx_ref, gp_ref, gs_ref, gr_ref,
           other, local, near, tots, totr, lasts, lastr, passed, wide, du_ref,
           pair_s, pair_r, rate_s, rate_r,
           s_other, s_near, s_far, s_tot, s_last, s_pass, s_pair, s_rate):
    span, width = x_ref.shape
    heads = raw_ref.shape[0]
    state = proj_ref.shape[1]
    chunks = width // CHUNK
    half = chunks // 2
    levels = seq_count.bit_length() - 1
    me = lax.axis_index("seq")
    core = lax.rem(me, 2)
    tensor = lax.axis_index("tensor")
    even = lax.rem(tensor, 2) == 0
    buddy = tensor + 1 - 2 * lax.rem(tensor, 2)

    def partner(bit):
        place = 2**bit
        upper = lax.rem(me // place, 2)
        return me + place - 2 * place * upper, upper

    barrier = pltpu.get_barrier_semaphore()
    for apart in range(1, seq_count):
        pl.semaphore_signal(barrier, inc=1, device_id={"seq": lax.rem(me + apart, seq_count)},
                            device_id_type=MESH)
    pl.semaphore_signal(barrier, inc=1, device_id={"tensor": buddy}, device_id_type=MESH)
    pl.semaphore_wait(barrier, seq_count)

    def send(src, dst, sems, at, **where):
        copy = pltpu.make_async_remote_copy(
            src_ref=src, dst_ref=dst, send_sem=sems.at[(0,) + at], recv_sem=sems.at[(1,) + at],
            device_id=where, device_id_type=MESH)
        copy.start()
        return copy

    swap = send(proj_ref, other, s_other, (), tensor=buddy)

    raw = raw_ref[...]
    small = jnp.exp(-jnp.abs(raw))
    one = 1.0 + small
    log1p = jnp.where(one == 1.0, small, jnp.log(one) * small / jnp.where(one == 1.0, 1.0, one - 1.0))
    step = jnp.maximum(raw, 0.0) + log1p
    sigmoid = jnp.where(raw >= 0, 1.0, small) / one
    rate = -jnp.exp(rate_ref[:, 0:1])
    log_decay = rate * step
    rows = lax.broadcasted_iota(jnp.int32, (span, span), 0)
    cols = lax.broadcasted_iota(jnp.int32, (span, span), 1)
    causal = cols >= rows
    cum = lax.dot_general(log_decay, causal.astype(F32), NN, precision=HIGHEST,
                          preferred_element_type=F32)
    total = cum[:, span - 1:span]
    at_row = lax.broadcasted_iota(jnp.int32, (heads, width), 0) * head_width
    at_col = lax.broadcasted_iota(jnp.int32, (heads, width), 1)
    spread = ((at_col >= at_row) & (at_col < at_row + head_width)).astype(F32).astype(BF16)
    spread3 = jnp.concatenate([spread, spread, spread], axis=0)

    def widen(a):
        high = a.astype(BF16)
        rest = a - high.astype(F32)
        mid = rest.astype(BF16)
        low = (rest - mid.astype(F32)).astype(BF16)
        return dot(jnp.concatenate([high, mid, low], axis=0), spread3, TN)

    def gather_heads(a):
        high = a.astype(BF16)
        rest = a - high.astype(F32)
        mid = rest.astype(BF16)
        return dot(spread, high, NT) + dot(spread, mid, NT)

    wide[0] = widen(step)
    wide[1] = widen(jnp.exp(total - cum))
    wide[2] = widen(jnp.exp(cum))
    swap.wait()
    own, theirs = proj_ref[...].astype(F32), other[...].astype(F32)
    b = jnp.where(even, own, theirs).astype(BF16)
    c = jnp.where(even, theirs, own).astype(BF16)

    for q in range(chunks):
        lanes = slice(q * CHUNK, (q + 1) * CHUNK)
        inj = x_ref[:, lanes].astype(F32) * wide[0, :, lanes] * wide[1, :, lanes]
        out = g_ref[:, lanes].astype(F32) * wide[2, :, lanes]
        high, low = split(inj)
        local[q, 0, :state] = dot(b, high, TN) + dot(b, low, TN)
        high, low = split(out)
        local[q, 1, :state] = dot(c, high, TN) + dot(c, low, TN)
        decay = jnp.broadcast_to(wide[2, span - 1:span, lanes], (8, CHUNK))
        local[q, 0, state:] = decay
        local[q, 1, state:] = decay

    mate, _ = partner(0)
    close = [send(local.at[(1 - core) * half + k], near.at[(1 - core) * half + k], s_near, (k,), seq=mate)
             for k in range(half)]
    rest = [send(local.at[core * half + k, core], near.at[core * half + k, core], s_far, (k,), seq=mate)
            for k in range(half)]

    is_up = core == 1

    def merge(up, f_own, r_own, d_own, f_in, r_in, d_in):
        f = jnp.where(up, 1.0, d_in) * f_own + jnp.where(up, d_own, 1.0) * f_in
        r = jnp.where(up, d_in, 1.0) * r_own + jnp.where(up, 1.0, d_own) * r_in
        return f, r, d_own * d_in

    sent = {}

    def put(level, k, f, r, d):
        target, upper = partner(level)
        d8 = jnp.broadcast_to(d, (8, CHUNK))
        if level == levels - 1:
            lasts[k, :state] = jnp.where(upper == 1, r, f)
            lasts[k, state:] = d8
            sent[level, k] = send(lasts.at[k], lastr.at[k], s_last, (k,), seq=target)
        else:
            tots[level - 1, k, 0, :state] = f
            tots[level - 1, k, 1, :state] = r
            tots[level - 1, k, 0, state:] = d8
            tots[level - 1, k, 1, state:] = d8
            sent[level, k] = send(tots.at[level - 1, k], totr.at[level - 1, k], s_tot,
                                  (level - 1, k), seq=target)

    for k in range(half):
        close[k].wait()
        q = core * half + k
        f, r, d = merge(is_up, local[q, 0, :state], local[q, 1, :state], local[q, 0, state:state + 1],
                        near[core * half + k, 0, :state], near[core * half + k, 1, :state],
                        near[core * half + k, 0, state:state + 1])
        put(1, k, f, r, d)

    scores = dot(b, c, NT)
    total_scores = jnp.zeros((span, span), F32)
    cum_t = jnp.transpose(cum)
    step_t = jnp.transpose(step)
    lane = lax.broadcasted_iota(jnp.int32, (span, 128), 1)
    per = 128 // head_width
    from_rows = []
    for p in range(width // 128):
        lanes = slice(p * 128, (p + 1) * 128)
        xs, gs = x_ref[:, lanes], g_ref[:, lanes]
        grown = jnp.zeros((span, 128), F32)
        for part in range(per):
            h = p * per + part
            mine = (lane >= part * head_width) & (lane < (part + 1) * head_width)
            inner = dot(jnp.where(mine, xs.astype(F32), 0.0).astype(BF16), gs, NT)
            gap = cum[h:h + 1, :] - cum_t[:, h:h + 1]
            fade = jnp.exp(jnp.where(causal, gap, -1e30))
            weight = fade * scores
            flow = inner * step_t[:, h:h + 1]
            total_scores = total_scores + flow * fade
            from_rows.append(jnp.sum(flow * weight, axis=0, keepdims=True))
            high, low = split(weight)
            grown = jnp.where(mine, dot(high, gs) + dot(low, gs), grown)
        du_ref[:, lanes] = grown
    row_part = jnp.concatenate(from_rows, axis=0)
    high, low = split(total_scores)
    grad_b = dot(high, c) + dot(low, c)
    grad_c = dot(high, b, TN) + dot(low, b, TN)

    zero = jnp.zeros((state, CHUNK), F32)
    ones = jnp.ones((1, CHUNK), F32)
    dp, dq = [ones] * half, [ones] * half
    for k in range(half):
        passed[core * half + k, 0] = zero
        passed[core * half + k, 1] = zero
    moved = []
    for level in range(1, levels):
        _, upper = partner(level)
        up = upper == 1
        for k in range(half):
            sent[level, k].wait()
            q = core * half + k
            if level == levels - 1:
                got = lastr[k, :state]
                before, after = passed[q, 0], passed[q, 1]
                passed[q, 0] = before + jnp.where(up, dp[k], 0.0) * got
                passed[q, 1] = after + jnp.where(up, 0.0, dq[k]) * got
                moved.append(send(passed.at[q], passed.at[q], s_pass, (k,), seq=mate))
            else:
                at = level - 1
                f_in, r_in = totr[at, k, 0, :state], totr[at, k, 1, :state]
                d_in = totr[at, k, 0, state:state + 1]
                passed[q, 0] = passed[q, 0] + jnp.where(up, dp[k], 0.0) * f_in
                passed[q, 1] = passed[q, 1] + jnp.where(up, 0.0, dq[k]) * r_in
                dp[k] = dp[k] * jnp.where(up, d_in, 1.0)
                dq[k] = dq[k] * jnp.where(up, 1.0, d_in)
                f, r, d = merge(up, tots[at, k, 0, :state], tots[at, k, 1, :state],
                                tots[at, k, 0, state:state + 1], f_in, r_in, d_in)
                put(level + 1, k, f, r, d)
    for copy in rest + moved:
        copy.wait()

    dcum = row_part
    last = []
    taken = []
    for q in range(chunks):
        lanes = slice(q * CHUNK, (q + 1) * CHUNK)
        before, after = passed[q, 0], passed[q, 1]
        side = near[q, 1 - core]
        joined = side[:state] + side[state:state + 1] * jnp.where(is_up, before, after)
        enter = jnp.where(is_up, joined, before)
        leave = jnp.where(is_up, after, joined)
        eh, el = split(enter)
        lh, ll = split(leave)
        xs, gs = x_ref[:, lanes].astype(F32), g_ref[:, lanes].astype(F32)
        step_w, end_w, cum_w = wide[0, :, lanes], wide[1, :, lanes], wide[2, :, lanes]
        carried = cum_w * (dot(c, eh) + dot(c, el))
        later = end_w * (dot(b, lh) + dot(b, ll))
        scaled = xs * step_w
        oh, ol = split(gs * cum_w)
        grad_c = grad_c + (dot(oh, eh, NT) + dot(oh, el, NT) + dot(ol, eh, NT))
        ih, il = split(scaled * end_w)
        grad_b = grad_b + (dot(ih, lh, NT) + dot(ih, ll, NT) + dot(il, lh, NT))
        du = du_ref[:, lanes] + later
        gx_ref[:, lanes] = (du * step_w).astype(BF16)
        last.append(jnp.sum(scaled * later, axis=0, keepdims=True)
                    + cum_w[span - 1:span] * jnp.sum(enter * leave, axis=0, keepdims=True))
        wide[2, :, lanes] = gs * carried
        du_ref[:, lanes] = du * xs
    mine = jnp.where(even, grad_b, grad_c)
    pair_s[...] = jnp.where(even, grad_c, grad_b)
    trade = send(pair_s, pair_r, s_pair, (), tensor=buddy)

    direct = gather_heads(du_ref[...])
    final = gather_heads(jnp.broadcast_to(jnp.concatenate(last, axis=1), (span, width)))
    dcum = row_part + gather_heads(wide[2]) - step * direct
    at_last = lax.broadcasted_iota(jnp.int32, (heads, span), 1) == span - 1
    dcum = dcum + jnp.where(at_last, final, 0.0)
    dlog = lax.dot_general(dcum, (rows >= cols).astype(F32), NN, precision=HIGHEST,
                           preferred_element_type=F32)
    rate_s[...] = jnp.broadcast_to(jnp.sum(dlog * log_decay, axis=1, keepdims=True), rate_s.shape)
    spreads = [send(rate_s, rate_r.at[apart - 1], s_rate, (apart - 1,),
                    seq=lax.rem(me + apart, seq_count)) for apart in range(1, seq_count)]
    gs_ref[...] = (direct + dlog * rate) * sigmoid
    trade.wait()
    gp_ref[...] = (mine + pair_r[...]).astype(BF16)
    summed = rate_s[...]
    for copy in spreads:
        copy.wait()
    for apart in range(1, seq_count):
        summed = summed + rate_r[apart - 1]
    gr_ref[...] = summed


def per_device(seq_count, inputs, projections, step_raw, rate_log, out_grad):
    _, span, width = inputs.shape
    heads = step_raw.shape[0]
    state = projections.shape[2]
    chunks = width // CHUNK
    half = chunks // 2
    levels = seq_count.bit_length() - 1
    dma = pltpu.SemaphoreType.DMA
    vmem = pl.BlockSpec(memory_space=pltpu.VMEM)
    tall = state + 8
    outs = pl.pallas_call(
        functools.partial(kernel, seq_count, width // heads),
        out_shape=(
            jax.ShapeDtypeStruct((span, width), BF16),
            jax.ShapeDtypeStruct((span, state), BF16),
            jax.ShapeDtypeStruct((heads, span), F32),
            jax.ShapeDtypeStruct((heads, 128), F32),
        ),
        in_specs=[vmem] * 5,
        out_specs=(vmem,) * 4,
        scratch_shapes=[
            pltpu.VMEM((span, state), BF16),
            pltpu.VMEM((chunks, 2, tall, CHUNK), F32),
            pltpu.VMEM((chunks, 2, tall, CHUNK), F32),
            pltpu.VMEM((max(levels - 2, 1), half, 2, tall, CHUNK), F32),
            pltpu.VMEM((max(levels - 2, 1), half, 2, tall, CHUNK), F32),
            pltpu.VMEM((half, tall, CHUNK), F32),
            pltpu.VMEM((half, tall, CHUNK), F32),
            pltpu.VMEM((chunks, 2, state, CHUNK), F32),
            pltpu.VMEM((3, span, width), F32),
            pltpu.VMEM((span, width), F32),
            pltpu.VMEM((span, state), F32),
            pltpu.VMEM((span, state), F32),
            pltpu.VMEM((heads, 128), F32),
            pltpu.VMEM((seq_count - 1, heads, 128), F32),
            dma((2,)),
            dma((2, half)),
            dma((2, half)),
            dma((2, max(levels - 2, 1), half)),
            dma((2, half)),
            dma((2, half)),
            dma((2,)),
            dma((2, seq_count - 1)),
        ],
        compiler_params=pltpu.CompilerParams(
            collective_id=0, has_side_effects=True, vmem_limit_bytes=56 * 2**20
        ),
    )(
        inputs.reshape(span, width),
        projections.reshape(span, state),
        step_raw.reshape(heads, span),
        jnp.broadcast_to(rate_log[:, None], (heads, 128)),
        out_grad.reshape(span, width),
    )
    gx, gp, gs, gr = outs
    return gx[None], gp[None], gs[:, None], gr[:, 0]


def solution(mesh):
    in_specs = (
        P(None, "seq", "tensor"),
        P(None, "seq", "tensor"),
        P("tensor", None, "seq"),
        P("tensor"),
        P(None, "seq", "tensor"),
    )
    out_specs = (
        P(None, "seq", "tensor"),
        P(None, "seq", "tensor"),
        P("tensor", None, "seq"),
        P("tensor"),
    )
    return jax.shard_map(
        functools.partial(per_device, mesh.shape["seq"]),
        mesh=mesh, in_specs=in_specs, out_specs=out_specs, check_vma=False,
    )
```

```python
import functools

import jax
import jax.numpy as jnp
from jax import lax
from jax.experimental import pallas as pl
from jax.experimental.pallas import tpu as pltpu
from jax.sharding import PartitionSpec as P

MESH = pl.DeviceIdType.MESH
HIGHEST = lax.Precision.HIGHEST
F32, BF16 = jnp.float32, jnp.bfloat16
CHUNK = 256
NT = (((1,), (1,)), ((), ()))
TN = (((0,), (0,)), ((), ()))
NN = (((1,), (0,)), ((), ()))


def dot(a, b, dims=NN):
    return lax.dot_general(a, b, dims, preferred_element_type=F32)


def split(a):
    high = a.astype(BF16)
    return high, (a - high.astype(F32)).astype(BF16)


def softplus(raw):
    small = jnp.exp(-jnp.abs(raw))
    one = 1.0 + small
    log1p = jnp.where(one == 1.0, small, jnp.log(one) * small / jnp.where(one == 1.0, 1.0, one - 1.0))
    return jnp.maximum(raw, 0.0) + log1p


def kernel(seq_count, head_width, x_ref, proj_ref, raw_ref, rate_ref, g_ref,
           gx_ref, gp_ref, gs_ref, gr_ref,
           other, stage, quad, pairs, raws, parts, outer, tots, totr, lasts, lastr, give, passed,
           wide, du_ref, pair_s, pair_r, rate_s, rate_r,
           s_other, s_first, s_second, s_proj, s_raw, s_tot, s_last, s_pass, s_pair, s_rate):
    span, width = x_ref.shape
    heads = raw_ref.shape[0]
    state = proj_ref.shape[1]
    chunks = width // CHUNK
    half = chunks // 2
    levels = seq_count.bit_length() - 1
    me = lax.axis_index("seq")
    core = lax.rem(me, 2)
    tensor = lax.axis_index("tensor")
    even = lax.rem(tensor, 2) == 0
    buddy = tensor + 1 - 2 * lax.rem(tensor, 2)

    def partner(bit):
        place = 2**bit
        upper = lax.rem(me // place, 2)
        return me + place - 2 * place * upper, upper

    barrier = pltpu.get_barrier_semaphore()
    for apart in range(1, seq_count):
        pl.semaphore_signal(barrier, inc=1, device_id={"seq": lax.rem(me + apart, seq_count)},
                            device_id_type=MESH)
    pl.semaphore_signal(barrier, inc=1, device_id={"tensor": buddy}, device_id_type=MESH)
    pl.semaphore_wait(barrier, seq_count)

    def send(src, dst, sems, at, **where):
        copy = pltpu.make_async_remote_copy(
            src_ref=src, dst_ref=dst, send_sem=sems.at[(0,) + at], recv_sem=sems.at[(1,) + at],
            device_id=where, device_id_type=MESH)
        copy.start()
        return copy

    swap = send(proj_ref, other, s_other, (), tensor=buddy)
    place = lax.rem(me, 4)
    base = me - place
    across = lax.rem(place // 2, 2)
    last_up = partner(levels - 1)[1]
    urgent = last_up
    side = width // 2
    raws[place] = raw_ref[...]
    for part in range(2):
        stage[part, 0] = x_ref[:, part * side:(part + 1) * side]
        stage[part, 1] = g_ref[:, part * side:(part + 1) * side]
    peers = []
    for flip in (2, 3, 1):
        there = place + (1 - 2 * lax.rem(place, 2)) * (flip % 2) + (2 - 4 * across) * (flip // 2)
        peers.append((flip - 1, base + there, lax.rem(there, 2)))
    first = [(send(raws.at[place], raws.at[place], s_raw, (i,), seq=to),
              send(stage.at[half_of, urgent], quad.at[place, urgent], s_first, (i,), seq=to))
             for i, to, half_of in peers]
    quad[place] = stage[core]

    raw = raw_ref[...]
    step = softplus(raw)
    sigmoid = 1.0 / (1.0 + jnp.exp(-raw))
    rate = -jnp.exp(rate_ref[:, 0:1])
    log_decay = rate * step
    rows = lax.broadcasted_iota(jnp.int32, (span, span), 0)
    cols = lax.broadcasted_iota(jnp.int32, (span, span), 1)
    causal = cols >= rows
    cum = lax.dot_general(log_decay, causal.astype(F32), NN, precision=HIGHEST,
                          preferred_element_type=F32)
    total = cum[:, span - 1:span]
    at_row = lax.broadcasted_iota(jnp.int32, (heads, width), 0) * head_width
    at_col = lax.broadcasted_iota(jnp.int32, (heads, width), 1)
    spread = ((at_col >= at_row) & (at_col < at_row + head_width)).astype(F32).astype(BF16)
    spread3 = jnp.concatenate([spread, spread, spread], axis=0)

    few_spread = spread[:heads // 2, :width // 2]
    few_spread3 = jnp.concatenate([few_spread, few_spread, few_spread], axis=0)

    def widen(a, by=spread3):
        high = a.astype(BF16)
        rest = a - high.astype(F32)
        mid = rest.astype(BF16)
        low = (rest - mid.astype(F32)).astype(BF16)
        return dot(jnp.concatenate([high, mid, low], axis=0), by, TN)

    def widen_half(a):
        return widen(a, few_spread3)

    def gather_heads(a):
        high = a.astype(BF16)
        rest = a - high.astype(F32)
        mid = rest.astype(BF16)
        return dot(spread, high, NT) + dot(spread, mid, NT)

    wide[0] = widen(step)
    wide[1] = widen(jnp.exp(total - cum))
    wide[2] = widen(jnp.exp(cum))
    swap.wait()
    own, theirs = proj_ref[...].astype(F32), other[...].astype(F32)
    b = jnp.where(even, own, theirs).astype(BF16)
    c = jnp.where(even, theirs, own).astype(BF16)

    pairs[place, 0] = b
    pairs[place, 1] = c
    second = [(send(pairs.at[place], pairs.at[place], s_proj, (i,), seq=to),
               send(stage.at[half_of, 1 - urgent], quad.at[place, 1 - urgent], s_second, (i,), seq=to))
              for i, to, half_of in peers]

    scores = dot(b, c, NT)
    total_scores = jnp.zeros((span, span), F32)
    cum_t = jnp.transpose(cum)
    step_t = jnp.transpose(step)
    lane = lax.broadcasted_iota(jnp.int32, (span, 128), 1)
    per = 128 // head_width
    from_rows = []
    for p in range(width // 128):
        lanes = slice(p * 128, (p + 1) * 128)
        xs, gs = x_ref[:, lanes], g_ref[:, lanes]
        grown = jnp.zeros((span, 128), F32)
        for part in range(per):
            h = p * per + part
            mine = (lane >= part * head_width) & (lane < (part + 1) * head_width)
            inner = dot(jnp.where(mine, xs.astype(F32), 0.0).astype(BF16), gs, NT)
            gap = cum[h:h + 1, :] - cum_t[:, h:h + 1]
            fade = jnp.exp(jnp.where(causal, gap, -1e30))
            weight = fade * scores
            flow = inner * step_t[:, h:h + 1]
            total_scores = total_scores + flow * fade
            from_rows.append(jnp.sum(flow * weight, axis=0, keepdims=True))
            high, low = split(weight)
            grown = jnp.where(mine, dot(high, gs) + dot(low, gs), grown)
        du_ref[:, lanes] = grown
    row_part = jnp.concatenate(from_rows, axis=0)
    high, low = split(total_scores)
    grad_b = dot(high, c) + dot(low, c)
    grad_c = dot(high, b, TN) + dot(low, b, TN)

    for copies in first:
        copies[0].wait()
    few = heads // 2
    wide_step, wide_cum, decays = [], [], []
    rate_half = jnp.where(core == 0, rate[:few], rate[few:])
    for r in range(4):
        step_r = softplus(jnp.where(core == 0, raws[r, :few], raws[r, few:]))
        cum_r = lax.dot_general(rate_half * step_r, causal.astype(F32), NN, precision=HIGHEST,
                                preferred_element_type=F32)
        wide_step.append((step_r, cum_r))
        decays.append(widen_half(jnp.exp(cum_r))[span - 1:span])

    def block_state(r, which):
        step_r, cum_r = wide_step[r]
        weight = jnp.where(which == 0, step_r * jnp.exp(cum_r[:, span - 1:span] - cum_r), jnp.exp(cum_r))
        high, low = split(quad[r, which].astype(F32) * widen_half(weight))
        basis = pairs[r, which]
        parts[r, which] = dot(basis, high, TN) + dot(basis, low, TN)

    def cut(row, k):
        return row[:, k * CHUNK:(k + 1) * CHUNK]

    def join(which, r, k):
        lanes = slice(k * CHUNK, (k + 1) * CHUNK)
        d0, d1 = cut(decays[r], k), cut(decays[r + 1], k)
        return (jnp.where(which == 0, d1, 1.0) * parts[r, which, :, lanes]
                + jnp.where(which == 0, 1.0, d0) * parts[r + 1, which, :, lanes])

    def whole(which, k):
        d01 = cut(decays[0], k) * cut(decays[1], k)
        d23 = cut(decays[2], k) * cut(decays[3], k)
        return (jnp.where(which == 0, d23, 1.0) * join(which, 0, k)
                + jnp.where(which == 0, 1.0, d01) * join(which, 2, k))

    def all_decay(k):
        return (cut(decays[0], k) * cut(decays[1], k)) * (cut(decays[2], k) * cut(decays[3], k))

    def merge(up, f_own, r_own, d_own, f_in, r_in, d_in):
        f = jnp.where(up, 1.0, d_in) * f_own + jnp.where(up, d_own, 1.0) * f_in
        r = jnp.where(up, d_in, 1.0) * r_own + jnp.where(up, 1.0, d_own) * r_in
        return f, r, d_own * d_in

    sent = {}

    def put_last(k, value):
        lasts[k] = value
        sent[levels - 1, k] = send(lasts.at[k], lastr.at[k], s_last, (k,), seq=partner(levels - 1)[0])

    def put(level, k, f, r, d):
        if level == levels - 1:
            put_last(k, jnp.where(last_up == 1, r, f))
        else:
            d8 = jnp.broadcast_to(d, (8, CHUNK))
            for i, value in enumerate((f, r)):
                tots[level - 2, k, i, :state] = value
                tots[level - 2, k, i, state:] = d8
            sent[level, k] = send(tots.at[level - 2, k], totr.at[level - 2, k], s_tot,
                                  (level - 2, k), seq=partner(level)[0])

    for copies in first:
        copies[1].wait()
    for copies in second:
        copies[0].wait()
    for r in range(4):
        block_state(r, urgent)
    if levels == 3:
        for k in range(half):
            put_last(k, whole(urgent, k))
    for copies in second:
        copies[1].wait()
    for r in range(4):
        block_state(r, 1 - urgent)
    if levels > 3:
        for k in range(half):
            put(2, k, whole(0, k), whole(1, k), all_decay(k))
        outer[...] = jnp.zeros_like(outer)

    mate, _ = partner(0)
    ones = jnp.ones((1, CHUNK), F32)
    dp, dq = [ones] * half, [ones] * half
    moved = []
    for level in range(2, levels):
        up = partner(level)[1] == 1
        for k in range(half):
            if level < levels - 1:
                sent[level, k].wait()
                at = level - 2
                f_in, r_in = totr[at, k, 0, :state], totr[at, k, 1, :state]
                d_in = totr[at, k, 0, state:state + 1]
                outer[k, 0] = outer[k, 0] + jnp.where(up, dp[k], 0.0) * f_in
                outer[k, 1] = outer[k, 1] + jnp.where(up, 0.0, dq[k]) * r_in
                dp[k] = dp[k] * jnp.where(up, d_in, 1.0)
                dq[k] = dq[k] * jnp.where(up, 1.0, d_in)
                f, r, d = merge(up, tots[at, k, 0, :state], tots[at, k, 1, :state],
                                tots[at, k, 0, state:state + 1], f_in, r_in, d_in)
                put(level + 1, k, f, r, d)
                continue
            right = across == 1
            lanes = slice(k * CHUNK, (k + 1) * CHUNK)
            d0, d1, d2, d3 = (cut(row, k) for row in decays)
            near0, near1 = jnp.where(right, d2, d0), jnp.where(right, d3, d1)
            enter0 = jnp.where(right, join(0, 0, k), 0.0)
            leave1 = jnp.where(right, 0.0, join(1, 2, k))
            sent[level, k].wait()
            got = lastr[k]
            before, after = jnp.where(up, dp[k], 0.0) * got, jnp.where(up, 0.0, dq[k]) * got
            if levels > 3:
                before, after = before + outer[k, 0], after + outer[k, 1]
            enter0 = enter0 + jnp.where(right, d0 * d1, 1.0) * before
            leave1 = leave1 + jnp.where(right, 1.0, d2 * d3) * after
            enter1 = near0 * enter0 + parts[2 * across, 0, :, lanes]
            leave0 = near1 * leave1 + parts[2 * across + 1, 1, :, lanes]
            odd = core == 1
            give[k, 0] = jnp.where(odd, enter0, enter1)
            give[k, 1] = jnp.where(odd, leave0, leave1)
            moved.append(send(give.at[k], passed.at[core * half + k], s_pass, (k,), seq=mate))
            passed[core * half + k, 0] = jnp.where(odd, enter1, enter0)
            passed[core * half + k, 1] = jnp.where(odd, leave1, leave0)
    for copy in moved:
        copy.wait()

    last = []
    for q in range(chunks):
        lanes = slice(q * CHUNK, (q + 1) * CHUNK)
        enter, leave = passed[q, 0], passed[q, 1]
        eh, el = split(enter)
        lh, ll = split(leave)
        xs, gs = x_ref[:, lanes].astype(F32), g_ref[:, lanes].astype(F32)
        step_w, end_w, cum_w = wide[0, :, lanes], wide[1, :, lanes], wide[2, :, lanes]
        carried = cum_w * (dot(c, eh) + dot(c, el))
        later = end_w * (dot(b, lh) + dot(b, ll))
        scaled = xs * step_w
        oh, ol = split(gs * cum_w)
        grad_c = grad_c + (dot(oh, eh, NT) + dot(oh, el, NT) + dot(ol, eh, NT))
        ih, il = split(scaled * end_w)
        grad_b = grad_b + (dot(ih, lh, NT) + dot(ih, ll, NT) + dot(il, lh, NT))
        du = du_ref[:, lanes] + later
        gx_ref[:, lanes] = (du * step_w).astype(BF16)
        last.append(jnp.sum(scaled * later, axis=0, keepdims=True)
                    + cum_w[span - 1:span] * jnp.sum(enter * leave, axis=0, keepdims=True))
        wide[2, :, lanes] = gs * carried
        du_ref[:, lanes] = du * xs
    mine = jnp.where(even, grad_b, grad_c)
    pair_s[...] = jnp.where(even, grad_c, grad_b)
    trade = send(pair_s, pair_r, s_pair, (), tensor=buddy)

    direct = gather_heads(du_ref[...])
    final = gather_heads(jnp.broadcast_to(jnp.concatenate(last, axis=1), (span, width)))
    dcum = row_part + gather_heads(wide[2]) - step * direct
    at_last = lax.broadcasted_iota(jnp.int32, (heads, span), 1) == span - 1
    dcum = dcum + jnp.where(at_last, final, 0.0)
    dlog = lax.dot_general(dcum, (rows >= cols).astype(F32), NN, precision=HIGHEST,
                           preferred_element_type=F32)
    rate_s[...] = jnp.broadcast_to(jnp.sum(dlog * log_decay, axis=1, keepdims=True), rate_s.shape)
    spreads = [send(rate_s, rate_r.at[apart - 1], s_rate, (apart - 1,),
                    seq=lax.rem(me + apart, seq_count)) for apart in range(1, seq_count)]
    gs_ref[...] = (direct + dlog * rate) * sigmoid
    trade.wait()
    gp_ref[...] = (mine + pair_r[...]).astype(BF16)
    summed = rate_s[...]
    for copy in spreads:
        copy.wait()
    for apart in range(1, seq_count):
        summed = summed + rate_r[apart - 1]
    gr_ref[...] = summed


def per_device(seq_count, inputs, projections, step_raw, rate_log, out_grad):
    _, span, width = inputs.shape
    heads = step_raw.shape[0]
    state = projections.shape[2]
    chunks = width // CHUNK
    half = chunks // 2
    levels = seq_count.bit_length() - 1
    dma = pltpu.SemaphoreType.DMA
    vmem = pl.BlockSpec(memory_space=pltpu.VMEM)
    tall = state + 8
    outs = pl.pallas_call(
        functools.partial(kernel, seq_count, width // heads),
        out_shape=(
            jax.ShapeDtypeStruct((span, width), BF16),
            jax.ShapeDtypeStruct((span, state), BF16),
            jax.ShapeDtypeStruct((heads, span), F32),
            jax.ShapeDtypeStruct((heads, 128), F32),
        ),
        in_specs=[vmem] * 5,
        out_specs=(vmem,) * 4,
        scratch_shapes=[
            pltpu.VMEM((span, state), BF16),
            pltpu.VMEM((2, 2, span, width // 2), BF16),
            pltpu.VMEM((4, 2, span, width // 2), BF16),
            pltpu.VMEM((4, 2, span, state), BF16),
            pltpu.VMEM((4, heads, span), F32),
            pltpu.VMEM((4, 2, state, width // 2), F32),
            pltpu.VMEM((half, 2, state, CHUNK), F32),
            pltpu.VMEM((max(levels - 3, 1), half, 2, tall, CHUNK), F32),
            pltpu.VMEM((max(levels - 3, 1), half, 2, tall, CHUNK), F32),
            pltpu.VMEM((half, state, CHUNK), F32),
            pltpu.VMEM((half, state, CHUNK), F32),
            pltpu.VMEM((half, 2, state, CHUNK), F32),
            pltpu.VMEM((chunks, 2, state, CHUNK), F32),
            pltpu.VMEM((3, span, width), F32),
            pltpu.VMEM((span, width), F32),
            pltpu.VMEM((span, state), F32),
            pltpu.VMEM((span, state), F32),
            pltpu.VMEM((heads, 128), F32),
            pltpu.VMEM((seq_count - 1, heads, 128), F32),
            dma((2,)),
            dma((2, 3)),
            dma((2, 3)),
            dma((2, 3)),
            dma((2, 3)),
            dma((2, max(levels - 3, 1), half)),
            dma((2, half)),
            dma((2, half)),
            dma((2,)),
            dma((2, seq_count - 1)),
        ],
        compiler_params=pltpu.CompilerParams(
            collective_id=0, has_side_effects=True, vmem_limit_bytes=56 * 2**20
        ),
    )(
        inputs.reshape(span, width),
        projections.reshape(span, state),
        step_raw.reshape(heads, span),
        jnp.broadcast_to(rate_log[:, None], (heads, 128)),
        out_grad.reshape(span, width),
    )
    gx, gp, gs, gr = outs
    return gx[None], gp[None], gs[:, None], gr[:, 0]


def solution(mesh):
    in_specs = (
        P(None, "seq", "tensor"),
        P(None, "seq", "tensor"),
        P("tensor", None, "seq"),
        P("tensor"),
        P(None, "seq", "tensor"),
    )
    out_specs = (
        P(None, "seq", "tensor"),
        P(None, "seq", "tensor"),
        P("tensor", None, "seq"),
        P("tensor"),
    )
    return jax.shard_map(
        functools.partial(per_device, mesh.shape["seq"]),
        mesh=mesh, in_specs=in_specs, out_specs=out_specs, check_vma=False,
    )
```

```python
import functools

import jax
import jax.numpy as jnp
from jax import lax
from jax.experimental import pallas as pl
from jax.experimental.pallas import tpu as pltpu
from jax.sharding import PartitionSpec as P

MESH = pl.DeviceIdType.MESH
HIGHEST = lax.Precision.HIGHEST
F32, BF16 = jnp.float32, jnp.bfloat16
CHUNK = 256
EARLY = 2
NT = (((1,), (1,)), ((), ()))
TN = (((0,), (0,)), ((), ()))
NN = (((1,), (0,)), ((), ()))


def dot(a, b, dims=NN):
    return lax.dot_general(a, b, dims, preferred_element_type=F32)


def split(a):
    high = a.astype(BF16)
    return high, (a - high.astype(F32)).astype(BF16)


def softplus(raw):
    small = jnp.exp(-jnp.abs(raw))
    one = 1.0 + small
    log1p = jnp.where(one == 1.0, small, jnp.log(one) * small / jnp.where(one == 1.0, 1.0, one - 1.0))
    return jnp.maximum(raw, 0.0) + log1p


def kernel(seq_count, head_width, x_ref, proj_ref, raw_ref, rate_ref, g_ref,
           gx_ref, gp_ref, gs_ref, gr_ref,
           other, stage, quad, pairs, raws, parts, outer, tots, totr, lasts, lastr, give, passed,
           wide, du_ref, pair_s, pair_r, rate_s, rate_r,
           s_other, s_first, s_second, s_proj, s_raw, s_tot, s_last, s_pass, s_pair, s_rate):
    span, width = x_ref.shape
    heads = raw_ref.shape[0]
    state = proj_ref.shape[1]
    chunks = width // CHUNK
    half = chunks // 2
    levels = seq_count.bit_length() - 1
    me = lax.axis_index("seq")
    core = lax.rem(me, 2)
    tensor = lax.axis_index("tensor")
    even = lax.rem(tensor, 2) == 0
    buddy = tensor + 1 - 2 * lax.rem(tensor, 2)

    def partner(bit):
        place = 2**bit
        upper = lax.rem(me // place, 2)
        return me + place - 2 * place * upper, upper

    barrier = pltpu.get_barrier_semaphore()
    for apart in range(1, seq_count):
        pl.semaphore_signal(barrier, inc=1, device_id={"seq": lax.rem(me + apart, seq_count)},
                            device_id_type=MESH)
    pl.semaphore_signal(barrier, inc=1, device_id={"tensor": buddy}, device_id_type=MESH)
    pl.semaphore_wait(barrier, seq_count)

    def send(src, dst, sems, at, **where):
        copy = pltpu.make_async_remote_copy(
            src_ref=src, dst_ref=dst, send_sem=sems.at[(0,) + at], recv_sem=sems.at[(1,) + at],
            device_id=where, device_id_type=MESH)
        copy.start()
        return copy

    swap = send(proj_ref, other, s_other, (), tensor=buddy)
    place = lax.rem(me, 4)
    base = me - place
    across = lax.rem(place // 2, 2)
    last_up = partner(levels - 1)[1]
    urgent = last_up
    raws[place] = raw_ref[...]
    for q in range(chunks):
        lanes = slice(q * CHUNK, (q + 1) * CHUNK)
        stage[q // half, q % half, 0] = x_ref[:, lanes]
        stage[q // half, q % half, 1] = g_ref[:, lanes]
    peers = []
    for flip in (2, 3, 1):
        there = place + (1 - 2 * lax.rem(place, 2)) * (flip % 2) + (2 - 4 * across) * (flip // 2)
        peers.append((flip - 1, base + there, lax.rem(there, 2)))
    news = [send(raws.at[place], raws.at[place], s_raw, (i,), seq=to) for i, to, _ in peers]

    def share(k, which, sems):
        return [send(stage.at[half_of, k, which], quad.at[place, k, which], sems, (k, i), seq=to)
                for i, to, half_of in peers]

    def share_basis(which, at):
        return [send(pairs.at[place, which], pairs.at[place, which], s_proj, (at, i), seq=to)
                for i, to, _ in peers]

    first, second = [share(0, urgent, s_first)], []
    quad[place] = stage[core]

    raw = raw_ref[...]
    step = softplus(raw)
    sigmoid = 1.0 / (1.0 + jnp.exp(-raw))
    head_row = lax.broadcasted_iota(jnp.int32, (heads, heads), 0)
    diagonal = head_row == lax.broadcasted_iota(jnp.int32, (heads, heads), 1)
    rate_row = jnp.broadcast_to(-jnp.exp(rate_ref[...]), (heads, heads))
    rate = jnp.sum(jnp.where(diagonal, rate_row, 0.0), axis=1, keepdims=True)
    log_decay = rate * step
    rows = lax.broadcasted_iota(jnp.int32, (span, span), 0)
    cols = lax.broadcasted_iota(jnp.int32, (span, span), 1)
    causal = cols >= rows
    cum = lax.dot_general(log_decay, causal.astype(F32), NN, precision=HIGHEST,
                          preferred_element_type=F32)
    total = cum[:, span - 1:span]
    at_row = lax.broadcasted_iota(jnp.int32, (heads, width), 0) * head_width
    at_col = lax.broadcasted_iota(jnp.int32, (heads, width), 1)
    spread = ((at_col >= at_row) & (at_col < at_row + head_width)).astype(F32).astype(BF16)
    spread3 = jnp.concatenate([spread, spread, spread], axis=0)

    few_spread = spread[:heads // 2, :width // 2]
    few_spread3 = jnp.concatenate([few_spread, few_spread, few_spread], axis=0)

    def widen(a, by=spread3):
        high = a.astype(BF16)
        rest = a - high.astype(F32)
        mid = rest.astype(BF16)
        low = (rest - mid.astype(F32)).astype(BF16)
        return dot(jnp.concatenate([high, mid, low], axis=0), by, TN)

    def widen_half(a):
        return widen(a, few_spread3)

    def gather_heads(a):
        high = a.astype(BF16)
        rest = a - high.astype(F32)
        mid = rest.astype(BF16)
        return dot(spread, high, NT) + dot(spread, mid, NT)

    wide[0] = widen(step)
    wide[1] = widen(jnp.exp(total - cum))
    wide[2] = widen(jnp.exp(cum))
    swap.wait()
    own, theirs = proj_ref[...].astype(F32), other[...].astype(F32)
    b = jnp.where(even, own, theirs).astype(BF16)
    c = jnp.where(even, theirs, own).astype(BF16)

    pairs[place, 0] = b
    pairs[place, 1] = c
    basis_first = share_basis(urgent, 0)
    first += [share(k, urgent, s_first) for k in range(1, half)]
    basis_second = share_basis(1 - urgent, 1)
    second = [share(k, 1 - urgent, s_second) for k in range(half)]

    scores = dot(b, c, NT)
    total_scores = jnp.zeros((span, span), F32)
    cum_t = jnp.transpose(cum)
    step_t = jnp.transpose(step)
    lane = lax.broadcasted_iota(jnp.int32, (span, 128), 1)
    per = 128 // head_width
    from_rows = []
    def inside(first_pair, end_pair, total_scores):
        for p in range(first_pair, end_pair):
            lanes = slice(p * 128, (p + 1) * 128)
            xs, gs = x_ref[:, lanes], g_ref[:, lanes]
            grown = jnp.zeros((span, 128), F32)
            for part in range(per):
                h = p * per + part
                mine = (lane >= part * head_width) & (lane < (part + 1) * head_width)
                inner = dot(jnp.where(mine, xs.astype(F32), 0.0).astype(BF16), gs, NT)
                gap = cum[h:h + 1, :] - cum_t[:, h:h + 1]
                fade = jnp.exp(jnp.where(causal, gap, -1e30))
                weight = fade * scores
                flow = inner * step_t[:, h:h + 1]
                total_scores = total_scores + flow * fade
                from_rows.append(jnp.sum(flow * weight, axis=0, keepdims=True))
                high, low = split(weight)
                grown = jnp.where(mine, dot(high, gs) + dot(low, gs), grown)
            du_ref[:, lanes] = grown
        return total_scores

    total_scores = inside(0, EARLY, total_scores)
    for copy in news:
        copy.wait()
    few = heads // 2
    wide_step, wide_cum, decays = [], [], []
    rate_half = jnp.where(core == 0, rate[:few], rate[few:])
    for r in range(4):
        step_r = softplus(jnp.where(core == 0, raws[r, :few], raws[r, few:]))
        cum_r = lax.dot_general(rate_half * step_r, causal.astype(F32), NN, precision=HIGHEST,
                                preferred_element_type=F32)
        wide_step.append((step_r, cum_r))
        decays.append(widen_half(jnp.exp(cum_r))[span - 1:span])

    def weigh(r, which):
        step_r, cum_r = wide_step[r]
        return widen_half(jnp.where(which == 0, step_r * jnp.exp(cum_r[:, span - 1:span] - cum_r),
                                    jnp.exp(cum_r)))

    urgent_weights = [weigh(r, urgent) for r in range(4)]

    def block_state(r, which, k, weight):
        lanes = slice(k * CHUNK, (k + 1) * CHUNK)
        high, low = split(quad[r, k, which].astype(F32) * weight[:, lanes])
        basis = pairs[r, which]
        parts[r, which, :, lanes] = dot(basis, high, TN) + dot(basis, low, TN)

    def cut(row, k):
        return row[:, k * CHUNK:(k + 1) * CHUNK]

    def join(which, r, k):
        lanes = slice(k * CHUNK, (k + 1) * CHUNK)
        d0, d1 = cut(decays[r], k), cut(decays[r + 1], k)
        return (jnp.where(which == 0, d1, 1.0) * parts[r, which, :, lanes]
                + jnp.where(which == 0, 1.0, d0) * parts[r + 1, which, :, lanes])

    def whole(which, k):
        d01 = cut(decays[0], k) * cut(decays[1], k)
        d23 = cut(decays[2], k) * cut(decays[3], k)
        return (jnp.where(which == 0, d23, 1.0) * join(which, 0, k)
                + jnp.where(which == 0, 1.0, d01) * join(which, 2, k))

    def all_decay(k):
        return (cut(decays[0], k) * cut(decays[1], k)) * (cut(decays[2], k) * cut(decays[3], k))

    def merge(up, f_own, r_own, d_own, f_in, r_in, d_in):
        f = jnp.where(up, 1.0, d_in) * f_own + jnp.where(up, d_own, 1.0) * f_in
        r = jnp.where(up, d_in, 1.0) * r_own + jnp.where(up, 1.0, d_own) * r_in
        return f, r, d_own * d_in

    sent = {}

    def put_last(k, value):
        lasts[k] = value
        sent[levels - 1, k] = send(lasts.at[k], lastr.at[k], s_last, (k,), seq=partner(levels - 1)[0])

    def put(level, k, f, r, d):
        if level == levels - 1:
            put_last(k, jnp.where(last_up == 1, r, f))
        else:
            d8 = jnp.broadcast_to(d, (8, CHUNK))
            for i, value in enumerate((f, r)):
                tots[level - 2, k, i, :state] = value
                tots[level - 2, k, i, state:] = d8
            sent[level, k] = send(tots.at[level - 2, k], totr.at[level - 2, k], s_tot,
                                  (level - 2, k), seq=partner(level)[0])

    for copy in basis_first:
        copy.wait()
    for k in range(half):
        for copy in first[k]:
            copy.wait()
        for r in range(4):
            block_state(r, urgent, k, urgent_weights[r])
        if levels == 3:
            put_last(k, whole(urgent, k))
    total_scores = inside(EARLY, width // 128, total_scores)
    row_part = jnp.concatenate(from_rows, axis=0)
    high, low = split(total_scores)
    grad_b = dot(high, c) + dot(low, c)
    grad_c = dot(high, b, TN) + dot(low, b, TN)
    weights = [weigh(r, 1 - urgent) for r in range(4)]
    for copy in basis_second:
        copy.wait()
    for k in range(half):
        for copy in second[k]:
            copy.wait()
        for r in range(4):
            block_state(r, 1 - urgent, k, weights[r])
    if levels > 3:
        for k in range(half):
            put(2, k, whole(0, k), whole(1, k), all_decay(k))
        outer[...] = jnp.zeros_like(outer)

    mate, _ = partner(0)
    ones = jnp.ones((1, CHUNK), F32)
    dp, dq = [ones] * half, [ones] * half
    moved = []
    for level in range(2, levels):
        up = partner(level)[1] == 1
        for k in range(half):
            if level < levels - 1:
                sent[level, k].wait()
                at = level - 2
                f_in, r_in = totr[at, k, 0, :state], totr[at, k, 1, :state]
                d_in = totr[at, k, 0, state:state + 1]
                outer[k, 0] = outer[k, 0] + jnp.where(up, dp[k], 0.0) * f_in
                outer[k, 1] = outer[k, 1] + jnp.where(up, 0.0, dq[k]) * r_in
                dp[k] = dp[k] * jnp.where(up, d_in, 1.0)
                dq[k] = dq[k] * jnp.where(up, 1.0, d_in)
                f, r, d = merge(up, tots[at, k, 0, :state], tots[at, k, 1, :state],
                                tots[at, k, 0, state:state + 1], f_in, r_in, d_in)
                put(level + 1, k, f, r, d)
                continue
            right = across == 1
            lanes = slice(k * CHUNK, (k + 1) * CHUNK)
            d0, d1, d2, d3 = (cut(row, k) for row in decays)
            near0, near1 = jnp.where(right, d2, d0), jnp.where(right, d3, d1)
            enter0 = jnp.where(right, join(0, 0, k), 0.0)
            leave1 = jnp.where(right, 0.0, join(1, 2, k))
            sent[level, k].wait()
            got = lastr[k]
            before, after = jnp.where(up, dp[k], 0.0) * got, jnp.where(up, 0.0, dq[k]) * got
            if levels > 3:
                before, after = before + outer[k, 0], after + outer[k, 1]
            enter0 = enter0 + jnp.where(right, d0 * d1, 1.0) * before
            leave1 = leave1 + jnp.where(right, 1.0, d2 * d3) * after
            enter1 = near0 * enter0 + parts[2 * across, 0, :, lanes]
            leave0 = near1 * leave1 + parts[2 * across + 1, 1, :, lanes]
            odd = core == 1
            give[k, 0] = jnp.where(odd, enter0, enter1)
            give[k, 1] = jnp.where(odd, leave0, leave1)
            moved.append(send(give.at[k], passed.at[core * half + k], s_pass, (k,), seq=mate))
            passed[core * half + k, 0] = jnp.where(odd, enter1, enter0)
            passed[core * half + k, 1] = jnp.where(odd, leave1, leave0)
    for copy in moved:
        copy.wait()

    last = []
    for q in range(chunks):
        lanes = slice(q * CHUNK, (q + 1) * CHUNK)
        enter, leave = passed[q, 0], passed[q, 1]
        eh, el = split(enter)
        lh, ll = split(leave)
        xs, gs = x_ref[:, lanes].astype(F32), g_ref[:, lanes].astype(F32)
        step_w, end_w, cum_w = wide[0, :, lanes], wide[1, :, lanes], wide[2, :, lanes]
        carried = cum_w * (dot(c, eh) + dot(c, el))
        later = end_w * (dot(b, lh) + dot(b, ll))
        scaled = xs * step_w
        oh, ol = split(gs * cum_w)
        grad_c = grad_c + (dot(oh, eh, NT) + dot(oh, el, NT) + dot(ol, eh, NT))
        ih, il = split(scaled * end_w)
        grad_b = grad_b + (dot(ih, lh, NT) + dot(ih, ll, NT) + dot(il, lh, NT))
        du = du_ref[:, lanes] + later
        gx_ref[:, lanes] = (du * step_w).astype(BF16)
        last.append(jnp.sum(scaled * later, axis=0, keepdims=True)
                    + cum_w[span - 1:span] * jnp.sum(enter * leave, axis=0, keepdims=True))
        wide[2, :, lanes] = gs * carried
        du_ref[:, lanes] = du * xs
    mine = jnp.where(even, grad_b, grad_c)
    pair_s[...] = jnp.where(even, grad_c, grad_b)
    trade = send(pair_s, pair_r, s_pair, (), tensor=buddy)

    direct = gather_heads(du_ref[...])
    final = gather_heads(jnp.broadcast_to(jnp.concatenate(last, axis=1), (span, width)))
    dcum = row_part + gather_heads(wide[2]) - step * direct
    at_last = lax.broadcasted_iota(jnp.int32, (heads, span), 1) == span - 1
    dcum = dcum + jnp.where(at_last, final, 0.0)
    dlog = lax.dot_general(dcum, (rows >= cols).astype(F32), NN, precision=HIGHEST,
                           preferred_element_type=F32)
    rate_s[...] = jnp.broadcast_to(jnp.sum(dlog * log_decay, axis=1, keepdims=True), rate_s.shape)
    spreads = [send(rate_s, rate_r.at[apart - 1], s_rate, (apart - 1,),
                    seq=lax.rem(me + apart, seq_count)) for apart in range(1, seq_count)]
    gs_ref[...] = (direct + dlog * rate) * sigmoid
    trade.wait()
    gp_ref[...] = (mine + pair_r[...]).astype(BF16)
    summed = rate_s[...]
    for copy in spreads:
        copy.wait()
    for apart in range(1, seq_count):
        summed = summed + rate_r[apart - 1]
    gr_ref[...] = jnp.sum(jnp.where(diagonal, summed[:, :heads], 0.0), axis=0, keepdims=True)


def per_device(seq_count, inputs, projections, step_raw, rate_log, out_grad):
    _, span, width = inputs.shape
    heads = step_raw.shape[0]
    state = projections.shape[2]
    chunks = width // CHUNK
    half = chunks // 2
    levels = seq_count.bit_length() - 1
    dma = pltpu.SemaphoreType.DMA
    vmem = pl.BlockSpec(memory_space=pltpu.VMEM)
    tall = state + 8
    outs = pl.pallas_call(
        functools.partial(kernel, seq_count, width // heads),
        out_shape=(
            jax.ShapeDtypeStruct((span, width), BF16),
            jax.ShapeDtypeStruct((span, state), BF16),
            jax.ShapeDtypeStruct((heads, span), F32),
            jax.ShapeDtypeStruct((1, heads), F32),
        ),
        in_specs=[vmem] * 5,
        out_specs=(vmem,) * 4,
        scratch_shapes=[
            pltpu.VMEM((span, state), BF16),
            pltpu.VMEM((2, half, 2, span, CHUNK), BF16),
            pltpu.VMEM((4, half, 2, span, CHUNK), BF16),
            pltpu.VMEM((4, 2, span, state), BF16),
            pltpu.VMEM((4, heads, span), F32),
            pltpu.VMEM((4, 2, state, width // 2), F32),
            pltpu.VMEM((half, 2, state, CHUNK), F32),
            pltpu.VMEM((max(levels - 3, 1), half, 2, tall, CHUNK), F32),
            pltpu.VMEM((max(levels - 3, 1), half, 2, tall, CHUNK), F32),
            pltpu.VMEM((half, state, CHUNK), F32),
            pltpu.VMEM((half, state, CHUNK), F32),
            pltpu.VMEM((half, 2, state, CHUNK), F32),
            pltpu.VMEM((chunks, 2, state, CHUNK), F32),
            pltpu.VMEM((3, span, width), F32),
            pltpu.VMEM((span, width), F32),
            pltpu.VMEM((span, state), F32),
            pltpu.VMEM((span, state), F32),
            pltpu.VMEM((heads, 128), F32),
            pltpu.VMEM((seq_count - 1, heads, 128), F32),
            dma((2,)),
            dma((2, half, 3)),
            dma((2, half, 3)),
            dma((2, 2, 3)),
            dma((2, 3)),
            dma((2, max(levels - 3, 1), half)),
            dma((2, half)),
            dma((2, half)),
            dma((2,)),
            dma((2, seq_count - 1)),
        ],
        compiler_params=pltpu.CompilerParams(
            collective_id=0, has_side_effects=True, vmem_limit_bytes=56 * 2**20
        ),
    )(
        inputs.reshape(span, width),
        projections.reshape(span, state),
        step_raw.reshape(heads, span),
        rate_log.reshape(1, heads),
        out_grad.reshape(span, width),
    )
    gx, gp, gs, gr = outs
    return gx[None], gp[None], gs[:, None], gr[0]


def solution(mesh):
    in_specs = (
        P(None, "seq", "tensor"),
        P(None, "seq", "tensor"),
        P("tensor", None, "seq"),
        P("tensor"),
        P(None, "seq", "tensor"),
    )
    out_specs = (
        P(None, "seq", "tensor"),
        P(None, "seq", "tensor"),
        P("tensor", None, "seq"),
        P("tensor"),
    )
    return jax.shard_map(
        functools.partial(per_device, mesh.shape["seq"]),
        mesh=mesh, in_specs=in_specs, out_specs=out_specs, check_vma=False,
    )
```

```python
import functools

import jax
import jax.numpy as jnp
from jax import lax
from jax.experimental import pallas as pl
from jax.experimental.pallas import tpu as pltpu
from jax.sharding import PartitionSpec as P

MESH = pl.DeviceIdType.MESH
HIGHEST = lax.Precision.HIGHEST
F32, BF16 = jnp.float32, jnp.bfloat16
CHUNK = 256
EARLY = 2
NT = (((1,), (1,)), ((), ()))
TN = (((0,), (0,)), ((), ()))
NN = (((1,), (0,)), ((), ()))


def dot(a, b, dims=NN):
    return lax.dot_general(a, b, dims, preferred_element_type=F32)


def split(a):
    high = a.astype(BF16)
    return high, (a - high.astype(F32)).astype(BF16)


def softplus(raw):
    small = jnp.exp(-jnp.abs(raw))
    one = 1.0 + small
    log1p = jnp.where(one == 1.0, small, jnp.log(one) * small / jnp.where(one == 1.0, 1.0, one - 1.0))
    return jnp.maximum(raw, 0.0) + log1p


def kernel(seq_count, head_width, x_ref, proj_ref, raw_ref, rate_ref, g_ref,
           gx_ref, gp_ref, gs_ref, gr_ref,
           other, stage, quad, pairs, raws, parts, outer, tots, totr, lasts, lastr, give, passed,
           wide, du_ref, pair_s, pair_r, rate_s, rate_r,
           s_other, s_first, s_second, s_proj, s_raw, s_tot, s_last, s_pass, s_pair, s_rate):
    span, width = x_ref.shape
    heads = raw_ref.shape[0]
    state = proj_ref.shape[1]
    chunks = width // CHUNK
    half = chunks // 2
    levels = seq_count.bit_length() - 1
    me = lax.axis_index("seq")
    core = lax.rem(me, 2)
    tensor = lax.axis_index("tensor")
    even = lax.rem(tensor, 2) == 0
    buddy = tensor + 1 - 2 * lax.rem(tensor, 2)

    def partner(bit):
        place = 2**bit
        upper = lax.rem(me // place, 2)
        return me + place - 2 * place * upper, upper

    barrier = pltpu.get_barrier_semaphore()
    for apart in range(1, seq_count):
        pl.semaphore_signal(barrier, inc=1, device_id={"seq": lax.rem(me + apart, seq_count)},
                            device_id_type=MESH)
    pl.semaphore_signal(barrier, inc=1, device_id={"tensor": buddy}, device_id_type=MESH)
    pl.semaphore_wait(barrier, seq_count)

    def send(src, dst, sems, at, **where):
        copy = pltpu.make_async_remote_copy(
            src_ref=src, dst_ref=dst, send_sem=sems.at[(0,) + at], recv_sem=sems.at[(1,) + at],
            device_id=where, device_id_type=MESH)
        copy.start()
        return copy

    swap = send(proj_ref, other, s_other, (), tensor=buddy)
    place = lax.rem(me, 4)
    base = me - place
    across = lax.rem(place // 2, 2)
    last_up = partner(levels - 1)[1]
    urgent = last_up
    raws[place] = raw_ref[...]
    for q in range(chunks):
        lanes = slice(q * CHUNK, (q + 1) * CHUNK)
        stage[q // half, q % half, 0] = x_ref[:, lanes]
        stage[q // half, q % half, 1] = g_ref[:, lanes]
    peers = []
    for flip in (2, 3, 1):
        there = place + (1 - 2 * lax.rem(place, 2)) * (flip % 2) + (2 - 4 * across) * (flip // 2)
        peers.append((flip - 1, base + there, lax.rem(there, 2)))
    news = [send(raws.at[place], raws.at[place], s_raw, (i,), seq=to) for i, to, _ in peers]

    def share(k, which, sems):
        return [send(stage.at[half_of, k, which], quad.at[place, k, which], sems, (k, i), seq=to)
                for i, to, half_of in peers]

    def share_basis(which, at):
        return [send(pairs.at[place, which], pairs.at[place, which], s_proj, (at, i), seq=to)
                for i, to, _ in peers]

    first, second = [share(0, urgent, s_first)], []
    quad[place] = stage[core]

    raw = raw_ref[...]
    step = softplus(raw)
    sigmoid = 1.0 / (1.0 + jnp.exp(-raw))
    head_row = lax.broadcasted_iota(jnp.int32, (heads, heads), 0)
    diagonal = head_row == lax.broadcasted_iota(jnp.int32, (heads, heads), 1)
    rate_row = jnp.broadcast_to(-jnp.exp(rate_ref[...]), (heads, heads))
    rate = jnp.sum(jnp.where(diagonal, rate_row, 0.0), axis=1, keepdims=True)
    log_decay = rate * step
    rows = lax.broadcasted_iota(jnp.int32, (span, span), 0)
    cols = lax.broadcasted_iota(jnp.int32, (span, span), 1)
    causal = cols >= rows
    cum = lax.dot_general(log_decay, causal.astype(F32), NN, precision=HIGHEST,
                          preferred_element_type=F32)
    total = cum[:, span - 1:span]
    at_row = lax.broadcasted_iota(jnp.int32, (heads, width), 0) * head_width
    at_col = lax.broadcasted_iota(jnp.int32, (heads, width), 1)
    spread = ((at_col >= at_row) & (at_col < at_row + head_width)).astype(F32).astype(BF16)
    spread3 = jnp.concatenate([spread, spread, spread], axis=0)

    few_spread = spread[:heads // 2, :width // 2]
    few_spread3 = jnp.concatenate([few_spread, few_spread, few_spread], axis=0)

    def widen(a, by=spread3):
        high = a.astype(BF16)
        rest = a - high.astype(F32)
        mid = rest.astype(BF16)
        low = (rest - mid.astype(F32)).astype(BF16)
        return dot(jnp.concatenate([high, mid, low], axis=0), by, TN)

    def widen_half(a):
        return widen(a, few_spread3)

    def gather_heads(a):
        high = a.astype(BF16)
        rest = a - high.astype(F32)
        mid = rest.astype(BF16)
        return dot(spread, high, NT) + dot(spread, mid, NT)

    wide[0] = widen(step)
    wide[1] = widen(jnp.exp(total - cum))
    wide[2] = widen(jnp.exp(cum))
    swap.wait()
    own, theirs = proj_ref[...].astype(F32), other[...].astype(F32)
    b = jnp.where(even, own, theirs).astype(BF16)
    c = jnp.where(even, theirs, own).astype(BF16)

    pairs[place, 0] = b
    pairs[place, 1] = c
    basis_first = share_basis(urgent, 0)
    first += [share(k, urgent, s_first) for k in range(1, half)]
    basis_second = share_basis(1 - urgent, 1)
    second = [share(k, 1 - urgent, s_second) for k in range(half)]

    scores = dot(b, c, NT)
    total_scores = jnp.zeros((span, span), F32)
    cum_t = jnp.transpose(cum)
    step_t = jnp.transpose(step)
    lane = lax.broadcasted_iota(jnp.int32, (span, 128), 1)
    per = 128 // head_width
    from_rows = []
    def inside(first_pair, end_pair, total_scores):
        for p in range(first_pair, end_pair):
            lanes = slice(p * 128, (p + 1) * 128)
            xs, gs = x_ref[:, lanes], g_ref[:, lanes]
            twice = jnp.concatenate([gs, gs], axis=0)
            grown = jnp.zeros((span, 128), F32)
            for part in range(per):
                h = p * per + part
                mine = (lane >= part * head_width) & (lane < (part + 1) * head_width)
                inner = dot(jnp.where(mine, xs.astype(F32), 0.0).astype(BF16), gs, NT)
                gap = cum[h:h + 1, :] - cum_t[:, h:h + 1]
                fade = jnp.exp(jnp.where(causal, gap, -1e30))
                weight = fade * scores
                flow = inner * step_t[:, h:h + 1]
                total_scores = total_scores + flow * fade
                from_rows.append(jnp.sum(flow * weight, axis=0, keepdims=True))
                high, low = split(weight)
                grown = jnp.where(mine, dot(jnp.concatenate([high, low], axis=1), twice), grown)
            du_ref[:, lanes] = grown
        return total_scores

    total_scores = inside(0, EARLY, total_scores)
    for copy in news:
        copy.wait()
    few = heads // 2
    wide_step = []
    rate_half = jnp.where(core == 0, rate[:few], rate[few:])
    for r in range(4):
        step_r = softplus(jnp.where(core == 0, raws[r, :few], raws[r, few:]))
        cum_r = lax.dot_general(rate_half * step_r, causal.astype(F32), NN, precision=HIGHEST,
                                preferred_element_type=F32)
        wide_step.append((step_r, cum_r))

    at_lane = lax.broadcasted_iota(jnp.int32, (few, span), 1)
    ends = wide_step[3][1][:, span - 1:span]
    for r in (2, 1, 0):
        ends = jnp.where(at_lane < (r + 1) * (span // 4), wide_step[r][1][:, span - 1:span], ends)
    ends = widen_half(jnp.exp(ends))
    decays = [ends[r * (span // 4):r * (span // 4) + 1] for r in range(4)]

    def weigh(r, which):
        step_r, cum_r = wide_step[r]
        return widen_half(jnp.where(which == 0, step_r * jnp.exp(cum_r[:, span - 1:span] - cum_r),
                                    jnp.exp(cum_r)))

    urgent_weights = [weigh(r, urgent) for r in range(4)]

    def block_state(r, which, k, weight, basis):
        lanes = slice(k * CHUNK, (k + 1) * CHUNK)
        high, low = split(quad[r, k, which].astype(F32) * weight[:, lanes])
        parts[r, which, :, lanes] = dot(basis, jnp.concatenate([high, low], axis=0))

    def turned(r, which):
        across_span = jnp.transpose(pairs[r, which])
        return jnp.concatenate([across_span, across_span], axis=1)

    def cut(row, k):
        return row[:, k * CHUNK:(k + 1) * CHUNK]

    def join(which, r, k):
        lanes = slice(k * CHUNK, (k + 1) * CHUNK)
        d0, d1 = cut(decays[r], k), cut(decays[r + 1], k)
        return (jnp.where(which == 0, d1, 1.0) * parts[r, which, :, lanes]
                + jnp.where(which == 0, 1.0, d0) * parts[r + 1, which, :, lanes])

    def whole(which, k):
        d01 = cut(decays[0], k) * cut(decays[1], k)
        d23 = cut(decays[2], k) * cut(decays[3], k)
        return (jnp.where(which == 0, d23, 1.0) * join(which, 0, k)
                + jnp.where(which == 0, 1.0, d01) * join(which, 2, k))

    def all_decay(k):
        return (cut(decays[0], k) * cut(decays[1], k)) * (cut(decays[2], k) * cut(decays[3], k))

    def merge(up, f_own, r_own, d_own, f_in, r_in, d_in):
        f = jnp.where(up, 1.0, d_in) * f_own + jnp.where(up, d_own, 1.0) * f_in
        r = jnp.where(up, d_in, 1.0) * r_own + jnp.where(up, 1.0, d_own) * r_in
        return f, r, d_own * d_in

    sent = {}

    def put_last(k, value):
        lasts[k] = value
        sent[levels - 1, k] = send(lasts.at[k], lastr.at[k], s_last, (k,), seq=partner(levels - 1)[0])

    def put(level, k, f, r, d):
        if level == levels - 1:
            put_last(k, jnp.where(last_up == 1, r, f))
        else:
            d8 = jnp.broadcast_to(d, (8, CHUNK))
            for i, value in enumerate((f, r)):
                tots[level - 2, k, i, :state] = value
                tots[level - 2, k, i, state:] = d8
            sent[level, k] = send(tots.at[level - 2, k], totr.at[level - 2, k], s_tot,
                                  (level - 2, k), seq=partner(level)[0])

    for copy in basis_first:
        copy.wait()
    bases = [turned(r, urgent) for r in range(4)]
    for k in range(half):
        for copy in first[k]:
            copy.wait()
        for r in range(4):
            block_state(r, urgent, k, urgent_weights[r], bases[r])
        if levels == 3:
            put_last(k, whole(urgent, k))
    total_scores = inside(EARLY, width // 128, total_scores)
    row_part = jnp.concatenate(from_rows, axis=0)
    high, low = split(total_scores)
    grad_b = dot(high, c) + dot(low, c)
    grad_c = dot(high, b, TN) + dot(low, b, TN)
    weights = [weigh(r, 1 - urgent) for r in range(4)]
    for copy in basis_second:
        copy.wait()
    bases = [turned(r, 1 - urgent) for r in range(4)]
    for k in range(half):
        for copy in second[k]:
            copy.wait()
        for r in range(4):
            block_state(r, 1 - urgent, k, weights[r], bases[r])
    if levels > 3:
        for k in range(half):
            put(2, k, whole(0, k), whole(1, k), all_decay(k))
        outer[...] = jnp.zeros_like(outer)

    last = [None] * chunks

    def finish(q, grad_b, grad_c):
        lanes = slice(q * CHUNK, (q + 1) * CHUNK)
        enter, leave = passed[q, 0], passed[q, 1]
        eh, el = split(enter)
        lh, ll = split(leave)
        xs, gs = x_ref[:, lanes].astype(F32), g_ref[:, lanes].astype(F32)
        step_w, end_w, cum_w = wide[0, :, lanes], wide[1, :, lanes], wide[2, :, lanes]
        carried = cum_w * (dot(c, eh) + dot(c, el))
        later = end_w * (dot(b, lh) + dot(b, ll))
        scaled = xs * step_w
        oh, ol = split(gs * cum_w)
        grad_c = grad_c + (dot(oh, eh, NT) + dot(oh, el, NT) + dot(ol, eh, NT))
        ih, il = split(scaled * end_w)
        grad_b = grad_b + (dot(ih, lh, NT) + dot(ih, ll, NT) + dot(il, lh, NT))
        du = du_ref[:, lanes] + later
        gx_ref[:, lanes] = (du * step_w).astype(BF16)
        last[q] = (jnp.sum(scaled * later, axis=0, keepdims=True)
                    + cum_w[span - 1:span] * jnp.sum(enter * leave, axis=0, keepdims=True))
        wide[2, :, lanes] = gs * carried
        du_ref[:, lanes] = du * xs
        return grad_b, grad_c

    mate, _ = partner(0)
    ones = jnp.ones((1, CHUNK), F32)
    dp, dq = [ones] * half, [ones] * half
    for level in range(2, levels):
        up = partner(level)[1] == 1
        for k in range(half):
            if level < levels - 1:
                sent[level, k].wait()
                at = level - 2
                f_in, r_in = totr[at, k, 0, :state], totr[at, k, 1, :state]
                d_in = totr[at, k, 0, state:state + 1]
                outer[k, 0] = outer[k, 0] + jnp.where(up, dp[k], 0.0) * f_in
                outer[k, 1] = outer[k, 1] + jnp.where(up, 0.0, dq[k]) * r_in
                dp[k] = dp[k] * jnp.where(up, d_in, 1.0)
                dq[k] = dq[k] * jnp.where(up, 1.0, d_in)
                f, r, d = merge(up, tots[at, k, 0, :state], tots[at, k, 1, :state],
                                tots[at, k, 0, state:state + 1], f_in, r_in, d_in)
                put(level + 1, k, f, r, d)
                continue
            right = across == 1
            lanes = slice(k * CHUNK, (k + 1) * CHUNK)
            d0, d1, d2, d3 = (cut(row, k) for row in decays)
            near0, near1 = jnp.where(right, d2, d0), jnp.where(right, d3, d1)
            enter0 = jnp.where(right, join(0, 0, k), 0.0)
            leave1 = jnp.where(right, 0.0, join(1, 2, k))
            sent[level, k].wait()
            got = lastr[k]
            before, after = jnp.where(up, dp[k], 0.0) * got, jnp.where(up, 0.0, dq[k]) * got
            if levels > 3:
                before, after = before + outer[k, 0], after + outer[k, 1]
            enter0 = enter0 + jnp.where(right, d0 * d1, 1.0) * before
            leave1 = leave1 + jnp.where(right, 1.0, d2 * d3) * after
            enter1 = near0 * enter0 + parts[2 * across, 0, :, lanes]
            leave0 = near1 * leave1 + parts[2 * across + 1, 1, :, lanes]
            odd = core == 1
            give[k, 0] = jnp.where(odd, enter0, enter1)
            give[k, 1] = jnp.where(odd, leave0, leave1)
            hand = send(give.at[k], passed.at[core * half + k], s_pass, (k,), seq=mate)
            passed[core * half + k, 0] = jnp.where(odd, enter1, enter0)
            passed[core * half + k, 1] = jnp.where(odd, leave1, leave0)
            hand.wait()
            for q in (k, half + k):
                grad_b, grad_c = finish(q, grad_b, grad_c)
    mine = jnp.where(even, grad_b, grad_c)
    pair_s[...] = jnp.where(even, grad_c, grad_b)
    trade = send(pair_s, pair_r, s_pair, (), tensor=buddy)

    direct = gather_heads(du_ref[...])
    final = gather_heads(jnp.broadcast_to(jnp.concatenate(last, axis=1), (span, width)))
    dcum = row_part + gather_heads(wide[2]) - step * direct
    at_last = lax.broadcasted_iota(jnp.int32, (heads, span), 1) == span - 1
    dcum = dcum + jnp.where(at_last, final, 0.0)
    dlog = lax.dot_general(dcum, (rows >= cols).astype(F32), NN, precision=HIGHEST,
                           preferred_element_type=F32)
    rate_s[...] = jnp.broadcast_to(jnp.sum(dlog * log_decay, axis=1, keepdims=True), rate_s.shape)
    spreads = [send(rate_s, rate_r.at[apart - 1], s_rate, (apart - 1,),
                    seq=lax.rem(me + apart, seq_count)) for apart in range(1, seq_count)]
    gs_ref[...] = (direct + dlog * rate) * sigmoid
    trade.wait()
    gp_ref[...] = (mine + pair_r[...]).astype(BF16)
    summed = rate_s[...]
    for copy in spreads:
        copy.wait()
    for apart in range(1, seq_count):
        summed = summed + rate_r[apart - 1]
    gr_ref[...] = jnp.sum(jnp.where(diagonal, summed[:, :heads], 0.0), axis=0, keepdims=True)


def per_device(seq_count, inputs, projections, step_raw, rate_log, out_grad):
    _, span, width = inputs.shape
    heads = step_raw.shape[0]
    state = projections.shape[2]
    chunks = width // CHUNK
    half = chunks // 2
    levels = seq_count.bit_length() - 1
    dma = pltpu.SemaphoreType.DMA
    vmem = pl.BlockSpec(memory_space=pltpu.VMEM)
    tall = state + 8
    outs = pl.pallas_call(
        functools.partial(kernel, seq_count, width // heads),
        out_shape=(
            jax.ShapeDtypeStruct((span, width), BF16),
            jax.ShapeDtypeStruct((span, state), BF16),
            jax.ShapeDtypeStruct((heads, span), F32),
            jax.ShapeDtypeStruct((1, heads), F32),
        ),
        in_specs=[vmem] * 5,
        out_specs=(vmem,) * 4,
        scratch_shapes=[
            pltpu.VMEM((span, state), BF16),
            pltpu.VMEM((2, half, 2, span, CHUNK), BF16),
            pltpu.VMEM((4, half, 2, span, CHUNK), BF16),
            pltpu.VMEM((4, 2, span, state), BF16),
            pltpu.VMEM((4, heads, span), F32),
            pltpu.VMEM((4, 2, state, width // 2), F32),
            pltpu.VMEM((half, 2, state, CHUNK), F32),
            pltpu.VMEM((max(levels - 3, 1), half, 2, tall, CHUNK), F32),
            pltpu.VMEM((max(levels - 3, 1), half, 2, tall, CHUNK), F32),
            pltpu.VMEM((half, state, CHUNK), F32),
            pltpu.VMEM((half, state, CHUNK), F32),
            pltpu.VMEM((half, 2, state, CHUNK), F32),
            pltpu.VMEM((chunks, 2, state, CHUNK), F32),
            pltpu.VMEM((3, span, width), F32),
            pltpu.VMEM((span, width), F32),
            pltpu.VMEM((span, state), F32),
            pltpu.VMEM((span, state), F32),
            pltpu.VMEM((heads, 128), F32),
            pltpu.VMEM((seq_count - 1, heads, 128), F32),
            dma((2,)),
            dma((2, half, 3)),
            dma((2, half, 3)),
            dma((2, 2, 3)),
            dma((2, 3)),
            dma((2, max(levels - 3, 1), half)),
            dma((2, half)),
            dma((2, half)),
            dma((2,)),
            dma((2, seq_count - 1)),
        ],
        compiler_params=pltpu.CompilerParams(
            collective_id=0, has_side_effects=True, vmem_limit_bytes=56 * 2**20
        ),
    )(
        inputs.reshape(span, width),
        projections.reshape(span, state),
        step_raw.reshape(heads, span),
        rate_log.reshape(1, heads),
        out_grad.reshape(span, width),
    )
    gx, gp, gs, gr = outs
    return gx[None], gp[None], gs[:, None], gr[0]


def solution(mesh):
    in_specs = (
        P(None, "seq", "tensor"),
        P(None, "seq", "tensor"),
        P("tensor", None, "seq"),
        P("tensor"),
        P(None, "seq", "tensor"),
    )
    out_specs = (
        P(None, "seq", "tensor"),
        P(None, "seq", "tensor"),
        P("tensor", None, "seq"),
        P("tensor"),
    )
    return jax.shard_map(
        functools.partial(per_device, mesh.shape["seq"]),
        mesh=mesh, in_specs=in_specs, out_specs=out_specs, check_vma=False,
    )
```

```python
import functools

import jax
import jax.numpy as jnp
from jax import lax
from jax.experimental import pallas as pl
from jax.experimental.pallas import tpu as pltpu
from jax.sharding import PartitionSpec as P

MESH = pl.DeviceIdType.MESH
HIGHEST = lax.Precision.HIGHEST
F32, BF16 = jnp.float32, jnp.bfloat16
CHUNK = 256
EARLY = 2
NT = (((1,), (1,)), ((), ()))
TN = (((0,), (0,)), ((), ()))
NN = (((1,), (0,)), ((), ()))


def dot(a, b, dims=NN):
    return lax.dot_general(a, b, dims, preferred_element_type=F32)


def split(a):
    high = a.astype(BF16)
    return high, (a - high.astype(F32)).astype(BF16)


def softplus(raw):
    small = jnp.exp(-jnp.abs(raw))
    one = 1.0 + small
    log1p = jnp.where(one == 1.0, small, jnp.log(one) * small / jnp.where(one == 1.0, 1.0, one - 1.0))
    return jnp.maximum(raw, 0.0) + log1p


def kernel(seq_count, head_width, x_ref, proj_ref, raw_ref, rate_ref, g_ref,
           gx_ref, gp_ref, gs_ref, gr_ref,
           other, stage, quad, pairs, raws, parts, outer, tots, totr, lasts, lastr, give, passed,
           wide, du_ref, pair_s, pair_r, rate_s, rate_r,
           s_other, s_first, s_second, s_proj, s_raw, s_tot, s_last, s_pass, s_pair, s_rate):
    span, width = x_ref.shape
    heads = raw_ref.shape[0]
    state = proj_ref.shape[1]
    chunks = width // CHUNK
    half = chunks // 2
    levels = seq_count.bit_length() - 1
    me = lax.axis_index("seq")
    core = lax.rem(me, 2)
    tensor = lax.axis_index("tensor")
    even = lax.rem(tensor, 2) == 0
    buddy = tensor + 1 - 2 * lax.rem(tensor, 2)

    def partner(bit):
        place = 2**bit
        upper = lax.rem(me // place, 2)
        return me + place - 2 * place * upper, upper

    barrier = pltpu.get_barrier_semaphore()
    for apart in range(1, seq_count):
        pl.semaphore_signal(barrier, inc=1, device_id={"seq": lax.rem(me + apart, seq_count)},
                            device_id_type=MESH)
    pl.semaphore_signal(barrier, inc=1, device_id={"tensor": buddy}, device_id_type=MESH)
    pl.semaphore_wait(barrier, seq_count)

    def send(src, dst, sems, at, **where):
        copy = pltpu.make_async_remote_copy(
            src_ref=src, dst_ref=dst, send_sem=sems.at[(0,) + at], recv_sem=sems.at[(1,) + at],
            device_id=where, device_id_type=MESH)
        copy.start()
        return copy

    swap = send(proj_ref, other, s_other, (), tensor=buddy)
    place = lax.rem(me, 4)
    base = me - place
    across = lax.rem(place // 2, 2)
    last_up = partner(levels - 1)[1]
    urgent = last_up
    raws[place] = raw_ref[...]
    for q in range(chunks):
        lanes = slice(q * CHUNK, (q + 1) * CHUNK)
        stage[q // half, q % half, 0] = x_ref[:, lanes]
        stage[q // half, q % half, 1] = g_ref[:, lanes]
    peers = []
    for flip in (2, 3, 1):
        there = place + (1 - 2 * lax.rem(place, 2)) * (flip % 2) + (2 - 4 * across) * (flip // 2)
        peers.append((flip - 1, base + there, lax.rem(there, 2)))
    news = [send(raws.at[place], raws.at[place], s_raw, (i,), seq=to) for i, to, _ in peers]

    def share(k, which, sems):
        return [send(stage.at[half_of, k, which], quad.at[place, k, which], sems, (k, i), seq=to)
                for i, to, half_of in peers]

    def share_basis(which, at):
        return [send(pairs.at[place, which], pairs.at[place, which], s_proj, (at, i), seq=to)
                for i, to, _ in peers if i != 2]

    def forward_basis(copies, which, at):
        copies[0].wait()
        facing = place + 2 - 4 * across
        return [send(pairs.at[facing, which], pairs.at[facing, which], s_proj, (at, 2), seq=peers[2][1]),
                copies[1]]

    first, second = [share(0, urgent, s_first)], []
    quad[place] = stage[core]

    raw = raw_ref[...]
    step = softplus(raw)
    sigmoid = 1.0 / (1.0 + jnp.exp(-raw))
    head_row = lax.broadcasted_iota(jnp.int32, (heads, heads), 0)
    diagonal = head_row == lax.broadcasted_iota(jnp.int32, (heads, heads), 1)
    rate_row = jnp.broadcast_to(-jnp.exp(rate_ref[...]), (heads, heads))
    rate = jnp.sum(jnp.where(diagonal, rate_row, 0.0), axis=1, keepdims=True)
    log_decay = rate * step
    rows = lax.broadcasted_iota(jnp.int32, (span, span), 0)
    cols = lax.broadcasted_iota(jnp.int32, (span, span), 1)
    causal = cols >= rows
    cum = lax.dot_general(log_decay, causal.astype(F32), NN, precision=HIGHEST,
                          preferred_element_type=F32)
    total = cum[:, span - 1:span]
    at_row = lax.broadcasted_iota(jnp.int32, (heads, width), 0) * head_width
    at_col = lax.broadcasted_iota(jnp.int32, (heads, width), 1)
    spread = ((at_col >= at_row) & (at_col < at_row + head_width)).astype(F32).astype(BF16)
    spread3 = jnp.concatenate([spread, spread, spread], axis=0)

    few_spread = spread[:heads // 2, :width // 2]
    few_spread3 = jnp.concatenate([few_spread, few_spread, few_spread], axis=0)

    def widen(a, by=spread3):
        high = a.astype(BF16)
        rest = a - high.astype(F32)
        mid = rest.astype(BF16)
        low = (rest - mid.astype(F32)).astype(BF16)
        return dot(jnp.concatenate([high, mid, low], axis=0), by, TN)

    def widen_half(a):
        return widen(a, few_spread3)

    def gather_heads(a):
        high = a.astype(BF16)
        rest = a - high.astype(F32)
        mid = rest.astype(BF16)
        return dot(spread, high, NT) + dot(spread, mid, NT)

    wide[0] = widen(step)
    wide[1] = widen(jnp.exp(total - cum))
    wide[2] = widen(jnp.exp(cum))
    swap.wait()
    own, theirs = proj_ref[...].astype(F32), other[...].astype(F32)
    b = jnp.where(even, own, theirs).astype(BF16)
    c = jnp.where(even, theirs, own).astype(BF16)

    pairs[place, 0] = b
    pairs[place, 1] = c
    basis_first = share_basis(urgent, 0)
    first += [share(k, urgent, s_first) for k in range(1, half)]
    basis_second = share_basis(1 - urgent, 1)
    second = [share(k, 1 - urgent, s_second) for k in range(half)]

    scores = dot(b, c, NT)
    total_scores = jnp.zeros((span, span), F32)
    cum_t = jnp.transpose(cum)
    step_t = jnp.transpose(step)
    lane = lax.broadcasted_iota(jnp.int32, (span, 128), 1)
    per = 128 // head_width
    from_rows = []
    def inside(first_pair, end_pair, total_scores):
        for p in range(first_pair, end_pair):
            lanes = slice(p * 128, (p + 1) * 128)
            xs, gs = x_ref[:, lanes], g_ref[:, lanes]
            twice = jnp.concatenate([gs, gs], axis=0)
            grown = jnp.zeros((span, 128), F32)
            for part in range(per):
                h = p * per + part
                mine = (lane >= part * head_width) & (lane < (part + 1) * head_width)
                inner = dot(jnp.where(mine, xs.astype(F32), 0.0).astype(BF16), gs, NT)
                gap = cum[h:h + 1, :] - cum_t[:, h:h + 1]
                fade = jnp.exp(jnp.where(causal, gap, -1e30))
                weight = fade * scores
                flow = inner * step_t[:, h:h + 1]
                total_scores = total_scores + flow * fade
                from_rows.append(jnp.sum(flow * weight, axis=0, keepdims=True))
                high, low = split(weight)
                grown = jnp.where(mine, dot(jnp.concatenate([high, low], axis=1), twice), grown)
            du_ref[:, lanes] = grown
        return total_scores

    total_scores = inside(0, EARLY, total_scores)
    for copy in news:
        copy.wait()
    few = heads // 2
    wide_step = []
    rate_half = jnp.where(core == 0, rate[:few], rate[few:])
    for r in range(4):
        step_r = softplus(jnp.where(core == 0, raws[r, :few], raws[r, few:]))
        cum_r = lax.dot_general(rate_half * step_r, causal.astype(F32), NN, precision=HIGHEST,
                                preferred_element_type=F32)
        wide_step.append((step_r, cum_r))

    at_lane = lax.broadcasted_iota(jnp.int32, (few, span), 1)
    ends = wide_step[3][1][:, span - 1:span]
    for r in (2, 1, 0):
        ends = jnp.where(at_lane < (r + 1) * (span // 4), wide_step[r][1][:, span - 1:span], ends)
    ends = widen_half(jnp.exp(ends))
    decays = [ends[r * (span // 4):r * (span // 4) + 1] for r in range(4)]

    def weigh(r, which):
        step_r, cum_r = wide_step[r]
        return widen_half(jnp.where(which == 0, step_r * jnp.exp(cum_r[:, span - 1:span] - cum_r),
                                    jnp.exp(cum_r)))

    urgent_weights = [weigh(r, urgent) for r in range(4)]

    def block_state(r, which, k, weight, basis):
        lanes = slice(k * CHUNK, (k + 1) * CHUNK)
        high, low = split(quad[r, k, which].astype(F32) * weight[:, lanes])
        parts[r, which, :, lanes] = dot(basis, jnp.concatenate([high, low], axis=0))

    def turned(r, which):
        across_span = jnp.transpose(pairs[r, which])
        return jnp.concatenate([across_span, across_span], axis=1)

    def cut(row, k):
        return row[:, k * CHUNK:(k + 1) * CHUNK]

    def join(which, r, k):
        lanes = slice(k * CHUNK, (k + 1) * CHUNK)
        d0, d1 = cut(decays[r], k), cut(decays[r + 1], k)
        return (jnp.where(which == 0, d1, 1.0) * parts[r, which, :, lanes]
                + jnp.where(which == 0, 1.0, d0) * parts[r + 1, which, :, lanes])

    def whole(which, k):
        d01 = cut(decays[0], k) * cut(decays[1], k)
        d23 = cut(decays[2], k) * cut(decays[3], k)
        return (jnp.where(which == 0, d23, 1.0) * join(which, 0, k)
                + jnp.where(which == 0, 1.0, d01) * join(which, 2, k))

    def all_decay(k):
        return (cut(decays[0], k) * cut(decays[1], k)) * (cut(decays[2], k) * cut(decays[3], k))

    def merge(up, f_own, r_own, d_own, f_in, r_in, d_in):
        f = jnp.where(up, 1.0, d_in) * f_own + jnp.where(up, d_own, 1.0) * f_in
        r = jnp.where(up, d_in, 1.0) * r_own + jnp.where(up, 1.0, d_own) * r_in
        return f, r, d_own * d_in

    sent = {}

    def put_last(k, value):
        lasts[k] = value
        sent[levels - 1, k] = send(lasts.at[k], lastr.at[k], s_last, (k,), seq=partner(levels - 1)[0])

    def put(level, k, f, r, d):
        if level == levels - 1:
            put_last(k, jnp.where(last_up == 1, r, f))
        else:
            d8 = jnp.broadcast_to(d, (8, CHUNK))
            for i, value in enumerate((f, r)):
                tots[level - 2, k, i, :state] = value
                tots[level - 2, k, i, state:] = d8
            sent[level, k] = send(tots.at[level - 2, k], totr.at[level - 2, k], s_tot,
                                  (level - 2, k), seq=partner(level)[0])

    for copy in forward_basis(basis_first, urgent, 0):
        copy.wait()
    bases = [turned(r, urgent) for r in range(4)]
    for k in range(half):
        for copy in first[k]:
            copy.wait()
        for r in range(4):
            block_state(r, urgent, k, urgent_weights[r], bases[r])
        if levels == 3:
            put_last(k, whole(urgent, k))
    basis_second = forward_basis(basis_second, 1 - urgent, 1)
    total_scores = inside(EARLY, width // 128, total_scores)
    row_part = jnp.concatenate(from_rows, axis=0)
    high, low = split(total_scores)
    grad_b = dot(high, c) + dot(low, c)
    grad_c = dot(high, b, TN) + dot(low, b, TN)
    weights = [weigh(r, 1 - urgent) for r in range(4)]
    for copy in basis_second:
        copy.wait()
    bases = [turned(r, 1 - urgent) for r in range(4)]
    for k in range(half):
        for copy in second[k]:
            copy.wait()
        for r in range(4):
            block_state(r, 1 - urgent, k, weights[r], bases[r])
    if levels > 3:
        for k in range(half):
            put(2, k, whole(0, k), whole(1, k), all_decay(k))
        outer[...] = jnp.zeros_like(outer)

    last = [None] * chunks

    def finish(q, grad_b, grad_c):
        lanes = slice(q * CHUNK, (q + 1) * CHUNK)
        enter, leave = passed[q, 0], passed[q, 1]
        eh, el = split(enter)
        lh, ll = split(leave)
        xs, gs = x_ref[:, lanes].astype(F32), g_ref[:, lanes].astype(F32)
        step_w, end_w, cum_w = wide[0, :, lanes], wide[1, :, lanes], wide[2, :, lanes]
        carried = cum_w * (dot(c, eh) + dot(c, el))
        later = end_w * (dot(b, lh) + dot(b, ll))
        scaled = xs * step_w
        oh, ol = split(gs * cum_w)
        grad_c = grad_c + (dot(oh, eh, NT) + dot(oh, el, NT) + dot(ol, eh, NT))
        ih, il = split(scaled * end_w)
        grad_b = grad_b + (dot(ih, lh, NT) + dot(ih, ll, NT) + dot(il, lh, NT))
        du = du_ref[:, lanes] + later
        gx_ref[:, lanes] = (du * step_w).astype(BF16)
        last[q] = (jnp.sum(scaled * later, axis=0, keepdims=True)
                    + cum_w[span - 1:span] * jnp.sum(enter * leave, axis=0, keepdims=True))
        wide[2, :, lanes] = gs * carried
        du_ref[:, lanes] = du * xs
        return grad_b, grad_c

    mate, _ = partner(0)
    ones = jnp.ones((1, CHUNK), F32)
    dp, dq = [ones] * half, [ones] * half
    for level in range(2, levels):
        up = partner(level)[1] == 1
        for k in range(half):
            if level < levels - 1:
                sent[level, k].wait()
                at = level - 2
                f_in, r_in = totr[at, k, 0, :state], totr[at, k, 1, :state]
                d_in = totr[at, k, 0, state:state + 1]
                outer[k, 0] = outer[k, 0] + jnp.where(up, dp[k], 0.0) * f_in
                outer[k, 1] = outer[k, 1] + jnp.where(up, 0.0, dq[k]) * r_in
                dp[k] = dp[k] * jnp.where(up, d_in, 1.0)
                dq[k] = dq[k] * jnp.where(up, 1.0, d_in)
                f, r, d = merge(up, tots[at, k, 0, :state], tots[at, k, 1, :state],
                                tots[at, k, 0, state:state + 1], f_in, r_in, d_in)
                put(level + 1, k, f, r, d)
                continue
            right = across == 1
            lanes = slice(k * CHUNK, (k + 1) * CHUNK)
            d0, d1, d2, d3 = (cut(row, k) for row in decays)
            near0, near1 = jnp.where(right, d2, d0), jnp.where(right, d3, d1)
            enter0 = jnp.where(right, join(0, 0, k), 0.0)
            leave1 = jnp.where(right, 0.0, join(1, 2, k))
            sent[level, k].wait()
            got = lastr[k]
            before, after = jnp.where(up, dp[k], 0.0) * got, jnp.where(up, 0.0, dq[k]) * got
            if levels > 3:
                before, after = before + outer[k, 0], after + outer[k, 1]
            enter0 = enter0 + jnp.where(right, d0 * d1, 1.0) * before
            leave1 = leave1 + jnp.where(right, 1.0, d2 * d3) * after
            enter1 = near0 * enter0 + parts[2 * across, 0, :, lanes]
            leave0 = near1 * leave1 + parts[2 * across + 1, 1, :, lanes]
            odd = core == 1
            give[k, 0] = jnp.where(odd, enter0, enter1)
            give[k, 1] = jnp.where(odd, leave0, leave1)
            hand = send(give.at[k], passed.at[core * half + k], s_pass, (k,), seq=mate)
            passed[core * half + k, 0] = jnp.where(odd, enter1, enter0)
            passed[core * half + k, 1] = jnp.where(odd, leave1, leave0)
            hand.wait()
            for q in (k, half + k):
                grad_b, grad_c = finish(q, grad_b, grad_c)
    mine = jnp.where(even, grad_b, grad_c)
    pair_s[...] = jnp.where(even, grad_c, grad_b)
    trade = send(pair_s, pair_r, s_pair, (), tensor=buddy)

    direct = gather_heads(du_ref[...])
    final = gather_heads(jnp.broadcast_to(jnp.concatenate(last, axis=1), (span, width)))
    dcum = row_part + gather_heads(wide[2]) - step * direct
    at_last = lax.broadcasted_iota(jnp.int32, (heads, span), 1) == span - 1
    dcum = dcum + jnp.where(at_last, final, 0.0)
    dlog = lax.dot_general(dcum, (rows >= cols).astype(F32), NN, precision=HIGHEST,
                           preferred_element_type=F32)
    rate_s[...] = jnp.broadcast_to(jnp.sum(dlog * log_decay, axis=1, keepdims=True), rate_s.shape)
    spreads = [send(rate_s, rate_r.at[apart - 1], s_rate, (apart - 1,),
                    seq=lax.rem(me + apart, seq_count)) for apart in range(1, seq_count)]
    gs_ref[...] = (direct + dlog * rate) * sigmoid
    trade.wait()
    gp_ref[...] = (mine + pair_r[...]).astype(BF16)
    summed = rate_s[...]
    for copy in spreads:
        copy.wait()
    for apart in range(1, seq_count):
        summed = summed + rate_r[apart - 1]
    gr_ref[...] = jnp.sum(jnp.where(diagonal, summed[:, :heads], 0.0), axis=0, keepdims=True)


def per_device(seq_count, inputs, projections, step_raw, rate_log, out_grad):
    _, span, width = inputs.shape
    heads = step_raw.shape[0]
    state = projections.shape[2]
    chunks = width // CHUNK
    half = chunks // 2
    levels = seq_count.bit_length() - 1
    dma = pltpu.SemaphoreType.DMA
    vmem = pl.BlockSpec(memory_space=pltpu.VMEM)
    tall = state + 8
    outs = pl.pallas_call(
        functools.partial(kernel, seq_count, width // heads),
        out_shape=(
            jax.ShapeDtypeStruct((span, width), BF16),
            jax.ShapeDtypeStruct((span, state), BF16),
            jax.ShapeDtypeStruct((heads, span), F32),
            jax.ShapeDtypeStruct((1, heads), F32),
        ),
        in_specs=[vmem] * 5,
        out_specs=(vmem,) * 4,
        scratch_shapes=[
            pltpu.VMEM((span, state), BF16),
            pltpu.VMEM((2, half, 2, span, CHUNK), BF16),
            pltpu.VMEM((4, half, 2, span, CHUNK), BF16),
            pltpu.VMEM((4, 2, span, state), BF16),
            pltpu.VMEM((4, heads, span), F32),
            pltpu.VMEM((4, 2, state, width // 2), F32),
            pltpu.VMEM((half, 2, state, CHUNK), F32),
            pltpu.VMEM((max(levels - 3, 1), half, 2, tall, CHUNK), F32),
            pltpu.VMEM((max(levels - 3, 1), half, 2, tall, CHUNK), F32),
            pltpu.VMEM((half, state, CHUNK), F32),
            pltpu.VMEM((half, state, CHUNK), F32),
            pltpu.VMEM((half, 2, state, CHUNK), F32),
            pltpu.VMEM((chunks, 2, state, CHUNK), F32),
            pltpu.VMEM((3, span, width), F32),
            pltpu.VMEM((span, width), F32),
            pltpu.VMEM((span, state), F32),
            pltpu.VMEM((span, state), F32),
            pltpu.VMEM((heads, 128), F32),
            pltpu.VMEM((seq_count - 1, heads, 128), F32),
            dma((2,)),
            dma((2, half, 3)),
            dma((2, half, 3)),
            dma((2, 2, 3)),
            dma((2, 3)),
            dma((2, max(levels - 3, 1), half)),
            dma((2, half)),
            dma((2, half)),
            dma((2,)),
            dma((2, seq_count - 1)),
        ],
        compiler_params=pltpu.CompilerParams(
            collective_id=0, has_side_effects=True, vmem_limit_bytes=56 * 2**20
        ),
    )(
        inputs.reshape(span, width),
        projections.reshape(span, state),
        step_raw.reshape(heads, span),
        rate_log.reshape(1, heads),
        out_grad.reshape(span, width),
    )
    gx, gp, gs, gr = outs
    return gx[None], gp[None], gs[:, None], gr[0]


def solution(mesh):
    in_specs = (
        P(None, "seq", "tensor"),
        P(None, "seq", "tensor"),
        P("tensor", None, "seq"),
        P("tensor"),
        P(None, "seq", "tensor"),
    )
    out_specs = (
        P(None, "seq", "tensor"),
        P(None, "seq", "tensor"),
        P("tensor", None, "seq"),
        P("tensor"),
    )
    return jax.shard_map(
        functools.partial(per_device, mesh.shape["seq"]),
        mesh=mesh, in_specs=in_specs, out_specs=out_specs, check_vma=False,
    )
```
